512 devices in a mesh: rep: 8 (over x, core), section: 8 (over z_lo), tp: 8 (over y, z_hi).
Axes of the slice: x: 4, y: 4, z: 16 (z_hi: 2, z_lo: 8; z = z_hi * 8 + z_lo), core: 2. Of those that a mesh axis runs over, the one named last changes fastest.
Arguments:
- cotangent: bfloat16 [1024, 6144], P('rep', ('section', 'tp')), may hold values from -6 to 6
- saved_inputs: bfloat16 [1024, 6144], P('rep', ('section', 'tp')), may hold values from -6 to 6
- up_weight: bfloat16 [6144, 24576], P('rep', ('section', 'tp')), may hold values from -0.078125 to 0.078125
- down_weight: bfloat16 [24576, 6144], P(('section', 'tp'), 'rep'), may hold values from -0.0390625 to 0.0390625
- block_owner: int32 [2, 8], replicated, may hold values from 0 to 7, each once within a row
Outputs:
- input_grads: bfloat16 [1024, 6144], P('rep', ('section', 'tp'))
- weight_grads: float32 [2, 8, 768, 24576], P(None, 'rep', None, ('section', 'tp'))
The draws below stay inside these ranges and needn't reach their ends.
Inputs may be any that keep to these rules, and one draw needn't show every extreme that they name: `block_owner`: each row is a permutation.
All inputs are finite; a program needn't handle non-finite values.
Results may differ from the reference program's by a relative error of at most 0.0034.
Values may be sent and summed in bfloat16 or wider, within the bound.
No kernel may reach another device: no remote copies, remote signals or barrier semaphores. Data moves between devices by JAX's collectives and lax.ppermute only.
A program may use at most 64 MiB of HBM per device.

```python
import math
import jax
import jax.numpy as jnp
from jax import lax

D = 6144
FF = 24576
TOKENS = 1024
BLOCK = 768
N_REP = 8


def shard_levels(rng, dims, shards, smallest, high):
    def one(dim, parts):
        steps = jax.random.uniform(jax.random.fold_in(jax.random.fold_in(rng, 6), dim), (parts,), jnp.float32, smallest / len(shards), high / len(shards))
        return jnp.repeat(jnp.exp(steps), dims[dim] // parts).reshape((-1,) + (1,) * (len(dims) - dim - 1))

    level = one(*shards[0])
    for cut in shards[1:]:
        level = level * one(*cut)
    return level


def gaussian(key, dims, deviation, limit, cuts=(), kind=jnp.bfloat16):
    result = jax.random.normal(key, dims, jnp.float32) * deviation
    if len(cuts) > 0:
        result = shard_levels(key, dims, cuts, -0.22, 0.18) * result
    return jnp.clip(result, min=-limit, max=limit).astype(kind)


def setup_inputs(seed: int = 0) -> dict:
    key_list = jax.random.split(jax.random.key(seed), 6)
    cotangent = gaussian(key_list[0], (TOKENS, D), 1.0, 6.0, ((0, 8), (1, 64)))
    saved_inputs = gaussian(key_list[1], (TOKENS, D), 1.0, 6.0, ((0, 8), (1, 64)))
    up_weight = gaussian(key_list[2], (D, FF), D ** -0.5, 0.078125, ((0, 8), (1, 64)))
    down_weight = gaussian(key_list[3], (FF, D), FF ** -0.5, 0.0390625, ((0, 64), (1, 8)))
    block_owner = jax.vmap(lambda own: jax.random.permutation(own, N_REP))(jax.random.split(key_list[4], 2)).reshape((2, N_REP)).astype(jnp.int32)
    return dict(cotangent=cotangent, saved_inputs=saved_inputs, up_weight=up_weight, down_weight=down_weight, block_owner=block_owner)


GELU_SCALE = math.sqrt(2.0 / math.pi)
GELU_CUBIC = 0.044715

def gelu_value(values):
    inner = GELU_SCALE * (values + GELU_CUBIC * values * values * values)
    return 0.5 * values * (1.0 + jnp.tanh(inner))

def gelu_deriv(values):
    tanh_part = jnp.tanh(GELU_SCALE * (values + GELU_CUBIC * values * values * values))
    return 0.5 * (1.0 + tanh_part) + 0.5 * values * (1.0 - tanh_part * tanh_part) * GELU_SCALE * (1.0 + 3.0 * GELU_CUBIC * values * values)

def reference(cotangent, saved_inputs, up_weight, down_weight, block_owner):
    pre_act = jnp.dot(saved_inputs, up_weight, preferred_element_type=jnp.float32)
    hidden = gelu_value(pre_act).astype(jnp.bfloat16)
    back_grad = jnp.dot(cotangent, down_weight.T, preferred_element_type=jnp.float32)
    dpre = (back_grad * gelu_deriv(pre_act)).astype(jnp.bfloat16)
    dx = jnp.dot(dpre, up_weight.T, preferred_element_type=jnp.float32)
    input_grads = (cotangent.astype(jnp.float32) + dx).astype(jnp.bfloat16)
    owners = jnp.arange(N_REP, dtype=jnp.int32)
    inverse = lax.optimization_barrier(jnp.sum(jnp.where(block_owner[:, None, :] == owners[None, :, None], owners[None, None, :], 0), axis=2)).astype(jnp.int32)
    up_grad = jnp.dot(saved_inputs.T, dpre, preferred_element_type=jnp.float32)
    up_part = jnp.take(up_grad.reshape(N_REP, BLOCK, FF), inverse[0], axis=0)
    down_grad = jnp.dot(cotangent.T, hidden, preferred_element_type=jnp.float32)
    down_part = jnp.take(down_grad.reshape(N_REP, BLOCK, FF), inverse[1], axis=0)
    weight_grads = jnp.stack([up_part, down_part])
    return (input_grads, weight_grads)
```

```python
import math

import jax
import jax.numpy as jnp
from jax import lax
from jax.sharding import Mesh
from jax.sharding import PartitionSpec as P

GELU_SCALE = math.sqrt(2.0 / math.pi)
GELU_CUBIC = 0.044715

REP = ("x", "core")
COL = ("section", "zh")
SHARD = ("section", "y", "zh")


def gelu_pair(values):
    tanh_part = jnp.tanh(GELU_SCALE * (values + GELU_CUBIC * values * values * values))
    value = 0.5 * values * (1.0 + tanh_part)
    deriv = 0.5 * (1.0 + tanh_part) + 0.5 * values * (1.0 - tanh_part * tanh_part) * GELU_SCALE * (
        1.0 + 3.0 * GELU_CUBIC * values * values
    )
    return value, deriv


def spread(block, axes, count):
    copies = lax.optimization_barrier(jnp.broadcast_to(block[None], (count,) + block.shape))
    return lax.all_to_all(copies, axes, split_axis=0, concat_axis=0, tiled=True)


def body(cotangent, saved_inputs, up_weight, down_weight, block_owner):
    n_rep = lax.axis_size(REP)
    n_col = lax.axis_size(COL)
    n_sec = lax.axis_size("section")
    n_y = lax.axis_size("y")
    n_zh = lax.axis_size("zh")
    tokens, width = cotangent.shape
    block = up_weight.shape[0]
    hidden_here = up_weight.shape[1]

    up_full = lax.all_gather(up_weight, REP, axis=0, tiled=True)
    down_full = lax.all_gather(down_weight, REP, axis=1, tiled=True)

    pair = jnp.stack([saved_inputs.T, cotangent.T])
    column = spread(pair, COL, n_col)
    column = column.reshape(n_sec, n_zh, 2, width, tokens)

    owners = jnp.arange(n_rep, dtype=jnp.int32)
    inverse = jnp.sum(
        jnp.where(block_owner[:, None, :] == owners[None, :, None], owners[None, None, :], 0),
        axis=2,
    )
    picked = jnp.stack(
        [jnp.take(column[:, :, j], inverse[j], axis=0) for j in range(2)], axis=1
    )
    owned = lax.all_to_all(picked, REP, split_axis=0, concat_axis=0, tiled=True)
    owned = owned.reshape(n_rep, 2, n_zh * width, tokens)
    owned = owned.transpose(1, 2, 0, 3).reshape(2, n_zh * width, n_rep * tokens)
    own_inputs = lax.all_gather(owned[0], "y", axis=0, tiled=True)
    own_grads = lax.all_gather(owned[1], "y", axis=0, tiled=True)

    full = spread(column, "y", n_y)
    full = full.transpose(3, 1, 0, 2, 4, 5).reshape(2, n_rep * block, tokens)

    pre_act = lax.dot_general(
        full[0], up_full, (((0,), (0,)), ((), ())), preferred_element_type=jnp.float32
    )
    back_grad = lax.dot_general(
        full[1], down_full, (((0,), (1,)), ((), ())), preferred_element_type=jnp.float32
    )
    value, deriv = gelu_pair(pre_act)
    hidden = value.astype(jnp.bfloat16)
    dpre = (back_grad * deriv).astype(jnp.bfloat16)

    both = lax.all_gather(jnp.concatenate([dpre, hidden], axis=1), REP, axis=0, tiled=True)

    partial_grad = lax.dot_general(
        up_full, dpre, (((1,), (1,)), ((), ())), preferred_element_type=jnp.float32
    ).astype(jnp.bfloat16)
    partial_grad = partial_grad.reshape(n_sec, n_y, n_zh * width, tokens).transpose(1, 0, 2, 3)
    parts = lax.all_to_all(partial_grad, "y", split_axis=0, concat_axis=0, tiled=True)
    parts = jnp.sum(parts.astype(jnp.float32), axis=0).astype(jnp.bfloat16)
    parts = parts.reshape(n_col, width, tokens)
    parts = lax.all_to_all(parts, COL, split_axis=0, concat_axis=0, tiled=True)
    summed = jnp.sum(parts.astype(jnp.float32), axis=0).T
    input_grads = (cotangent.astype(jnp.float32) + summed).astype(jnp.bfloat16)

    up_block = jnp.dot(own_inputs, both[:, :hidden_here], preferred_element_type=jnp.float32)
    down_block = jnp.dot(own_grads, both[:, hidden_here:], preferred_element_type=jnp.float32)
    weight_grads = jnp.stack([up_block, down_block])[:, None]
    return (input_grads, weight_grads)


def solution(mesh):
    fine = Mesh(mesh.devices.reshape(4, 2, 8, 4, 2), ("x", "core", "section", "y", "zh"))
    in_specs = (
        P(REP, SHARD),
        P(REP, SHARD),
        P(REP, SHARD),
        P(SHARD, REP),
        P(),
    )
    out_specs = (P(REP, SHARD), P(None, REP, None, SHARD))
    return jax.shard_map(body, mesh=fine, in_specs=in_specs, out_specs=out_specs, check_vma=False)
```

```python
import math

import jax
import jax.numpy as jnp
from jax import lax
from jax.sharding import Mesh
from jax.sharding import PartitionSpec as P

GELU_SCALE = math.sqrt(2.0 / math.pi)
GELU_CUBIC = 0.044715

REP = ("x", "core")
SHARD = ("sh", "sl", "y", "zh")


def gelu_pair(values):
    tanh_part = jnp.tanh(GELU_SCALE * (values + GELU_CUBIC * values * values * values))
    value = 0.5 * values * (1.0 + tanh_part)
    deriv = 0.5 * (1.0 + tanh_part) + 0.5 * values * (1.0 - tanh_part * tanh_part) * GELU_SCALE * (
        1.0 + 3.0 * GELU_CUBIC * values * values
    )
    return value, deriv


def spread(block, axes, count):
    copies = lax.optimization_barrier(jnp.broadcast_to(block[None], (count,) + block.shape))
    return lax.all_to_all(copies, axes, split_axis=0, concat_axis=0, tiled=True)


def shift(block, axis, step):
    size = lax.axis_size(axis)
    return lax.ppermute(block, axis, [(i, (i + step) % size) for i in range(size)])


def body(cotangent, saved_inputs, up_weight, down_weight, block_owner):
    n_x = lax.axis_size("x")
    n_core = lax.axis_size("core")
    n_rep = n_x * n_core
    n_sh = lax.axis_size("sh")
    n_sl = lax.axis_size("sl")
    n_y = lax.axis_size("y")
    n_zh = lax.axis_size("zh")
    tokens, width = cotangent.shape
    block = up_weight.shape[0]
    hidden_here = up_weight.shape[1]

    up_full = lax.all_gather(up_weight, REP, axis=0, tiled=True)
    down_full = lax.all_gather(down_weight, REP, axis=1, tiled=True)

    pair = jnp.stack([saved_inputs.T, cotangent.T])
    spaced = spread(pair, ("sh", "zh"), n_sh * n_zh)
    column = lax.all_gather(spaced, "sl", axis=0, tiled=False)
    full = spread(column, "y", n_y)
    full = full.reshape(n_y, n_sl, n_sh, n_zh, 2, width, tokens)
    full = full.transpose(4, 2, 1, 0, 3, 5, 6).reshape(2, n_rep, block, tokens)

    owners = jnp.arange(n_rep, dtype=jnp.int32)
    inverse = jnp.sum(
        jnp.where(block_owner[:, None, :] == owners[None, :, None], owners[None, None, :], 0),
        axis=2,
    )
    here = lax.axis_index("x")
    core = lax.axis_index("core")
    steps = jnp.arange(n_x, dtype=jnp.int32)
    ahead = ((here + steps) % n_x) * n_core
    keep, give = (
        jnp.stack(
            [jnp.take(full[j], jnp.take(inverse[j], ahead + c), axis=0) for j in range(2)], axis=1
        )
        for c in (core, 1 - core)
    )
    got = shift(give, "core", 1)
    message = jnp.stack([jnp.where(core == 0, keep, got), jnp.where(core == 0, got, keep)], axis=1)
    owned = [message[0]] + [shift(message[k], "x", k) for k in range(1, n_x)]

    flat = full.reshape(2, n_rep * block, tokens)
    pre_act = lax.dot_general(
        flat[0], up_full, (((0,), (0,)), ((), ())), preferred_element_type=jnp.float32
    )
    back_grad = lax.dot_general(
        flat[1], down_full, (((0,), (1,)), ((), ())), preferred_element_type=jnp.float32
    )
    value, deriv = gelu_pair(pre_act)
    hidden = value.astype(jnp.bfloat16)
    dpre = (back_grad * deriv).astype(jnp.bfloat16)

    both = lax.all_gather(jnp.concatenate([dpre, hidden], axis=1), REP, axis=0, tiled=True)

    partial_grad = lax.dot_general(
        up_full, dpre, (((1,), (1,)), ((), ())), preferred_element_type=jnp.float32
    ).astype(jnp.bfloat16)
    partial_grad = partial_grad.reshape(n_sh, n_sl, n_y, n_zh, width, tokens)
    partial_grad = partial_grad.transpose(2, 0, 1, 3, 4, 5).reshape(n_y, -1, width, tokens)
    parts = lax.all_to_all(partial_grad, "y", split_axis=0, concat_axis=0, tiled=True)
    parts = jnp.sum(parts.astype(jnp.float32), axis=0).astype(jnp.bfloat16)
    parts = lax.all_to_all(parts, ("sh", "sl", "zh"), split_axis=0, concat_axis=0, tiled=True)
    summed = jnp.sum(parts.astype(jnp.float32), axis=0).T
    input_grads = (cotangent.astype(jnp.float32) + summed).astype(jnp.bfloat16)

    rows = n_core * tokens
    ordered = jnp.take(
        both.reshape(n_x, rows, 2 * hidden_here), (here - steps) % n_x, axis=0
    ).reshape(n_x * rows, 2 * hidden_here)
    own_inputs, own_grads = (
        jnp.concatenate([owned[k][c, j] for k in range(n_x) for c in range(n_core)], axis=1)
        for j in range(2)
    )
    up_block = jnp.dot(own_inputs, ordered[:, :hidden_here], preferred_element_type=jnp.float32)
    down_block = jnp.dot(own_grads, ordered[:, hidden_here:], preferred_element_type=jnp.float32)
    weight_grads = jnp.stack([up_block, down_block])[:, None]
    return (input_grads, weight_grads)


def solution(mesh):
    fine = Mesh(mesh.devices.reshape(4, 2, 2, 4, 4, 2), ("x", "core", "sh", "sl", "y", "zh"))
    in_specs = (
        P(REP, SHARD),
        P(REP, SHARD),
        P(REP, SHARD),
        P(SHARD, REP),
        P(),
    )
    out_specs = (P(REP, SHARD), P(None, REP, None, SHARD))
    return jax.shard_map(body, mesh=fine, in_specs=in_specs, out_specs=out_specs, check_vma=False)
```

```python
import math

import jax
import jax.numpy as jnp
from jax import lax
from jax.experimental import pallas as pl
from jax.experimental.pallas import tpu as pltpu
from jax.sharding import Mesh
from jax.sharding import PartitionSpec as P

GELU_SCALE = math.sqrt(2.0 / math.pi)
GELU_CUBIC = 0.044715

REP = ("x", "core")
SHARD = ("sh", "sl", "y", "zh")


def gelu_pair(values):
    tanh_part = jnp.tanh(GELU_SCALE * (values + GELU_CUBIC * values * values * values))
    value = 0.5 * values * (1.0 + tanh_part)
    deriv = 0.5 * (1.0 + tanh_part) + 0.5 * values * (1.0 - tanh_part * tanh_part) * GELU_SCALE * (
        1.0 + 3.0 * GELU_CUBIC * values * values
    )
    return value, deriv


def spread(block, axes, count):
    copies = lax.optimization_barrier(jnp.broadcast_to(block[None], (count,) + block.shape))
    return lax.all_to_all(copies, axes, split_axis=0, concat_axis=0, tiled=True)


def shift(block, axis, step):
    size = lax.axis_size(axis)
    return lax.ppermute(block, axis, [(i, (i + step) % size) for i in range(size)])


def end_of(position, e):
    return jnp.where(e == 0, position[1], 1 - position[1])


def arrange_kernel(steps, owner, position, plain, *refs):
    del owner, position
    chosen, flats, messages = refs[:steps], refs[steps : steps + 2], refs[steps + 2 :]
    for j in range(2):

        @pl.when(pl.program_id(0) == j)
        def _(j=j):
            for b in range(plain.shape[1]):
                flats[j][b] = plain[:, b, 0, :, 0]

    for k in range(steps):
        messages[k][0, 0] = chosen[k][:, 0, 0, :, 0]


def arrange(gathered, owner, position, n_x, n_core):
    n_y, n_sl, n_sh, n_zh, _, width, tokens = gathered.shape
    n_blocks = n_sl * n_sh
    piece = (n_y, 1, 1, n_zh, 1, width, tokens)

    def chosen_at(k):
        def index(j, e, owner, position):
            target = lax.rem(position[0] + k, n_x) * n_core + end_of(position, e)
            b = sum(jnp.where(owner[j, i] == target, i, 0) for i in range(n_blocks))
            return (0, lax.rem(b, n_sl), lax.div(b, n_sl), 0, j, 0, 0)

        return index

    out = (n_y, n_zh, width, tokens)
    return pl.pallas_call(
        lambda *refs: arrange_kernel(n_x, *refs),
        grid_spec=pltpu.PrefetchScalarGridSpec(
            num_scalar_prefetch=2,
            grid=(2, n_sh),
            in_specs=[
                pl.BlockSpec(
                    (n_y, n_sl, 1, n_zh, 1, width, tokens), lambda j, h, *_: (0, 0, h, 0, j, 0, 0)
                )
            ]
            + [pl.BlockSpec(piece, chosen_at(k)) for k in range(n_x)],
            out_specs=[
                pl.BlockSpec(
                    (n_sl,) + out, lambda j, h, *_: (jnp.where(j == 0, h, n_sh - 1), 0, 0, 0, 0)
                ),
                pl.BlockSpec((n_sl,) + out, lambda j, h, *_: (jnp.where(j == 0, 0, h), 0, 0, 0, 0)),
            ]
            + [pl.BlockSpec((1, 1) + out, lambda j, e, *_: (e, j, 0, 0, 0, 0))] * n_x,
        ),
        out_shape=[jax.ShapeDtypeStruct((n_blocks,) + out, gathered.dtype)] * 2
        + [jax.ShapeDtypeStruct((n_core, 2) + out, gathered.dtype)] * n_x,
        compiler_params=pltpu.CompilerParams(vmem_limit_bytes=24 * 1024 * 1024),
        cost_estimate=pl.CostEstimate(
            flops=0, bytes_accessed=8 * gathered.size, transcendentals=0
        ),
    )(owner, position, gathered, *([gathered] * n_x))


def collect_kernel(steps, *refs):
    for k in range(steps):
        refs[-1][k, 0] = refs[k][0, 0]


def collect(pieces, after):
    steps = len(pieces)
    rows, tokens = pieces[0].shape[2:]
    return pl.pallas_call(
        lambda *refs: collect_kernel(steps, *refs),
        grid=(2,),
        in_specs=[pl.BlockSpec((1, 1, rows, tokens), lambda j: (1, j, 0, 0))] * steps
        + [pl.BlockSpec(memory_space=pl.ANY)],
        out_specs=pl.BlockSpec((steps, 1, rows, tokens), lambda j: (0, j, 0, 0)),
        out_shape=jax.ShapeDtypeStruct((steps, 2, rows, tokens), pieces[0].dtype),
        compiler_params=pltpu.CompilerParams(vmem_limit_bytes=24 * 1024 * 1024),
        cost_estimate=pl.CostEstimate(
            flops=0, bytes_accessed=8 * steps * rows * tokens, transcendentals=0
        ),
    )(*pieces, after)


def grads_kernel(steps, n_core, position, *refs):
    mine, (theirs, both, out) = refs[:steps], refs[steps:]
    total = None
    for k in range(steps):
        row = lax.rem(position[0] + (steps - k), steps) * n_core
        left = jnp.concatenate([mine[k][0, 0], theirs[k, 0]], axis=1)
        right = jnp.concatenate([both[row + position[1]], both[row + 1 - position[1]]], axis=0)
        term = jnp.dot(left, right, preferred_element_type=jnp.float32)
        total = term if total is None else total + term
    out[0, 0] = total


def block_grads(mine, theirs, both, position, n_core):
    steps = len(mine)
    rows, tokens = mine[0].shape[2:]
    groups, _, columns = both.shape
    hidden_here = columns // 2
    return pl.pallas_call(
        lambda *refs: grads_kernel(steps, n_core, *refs),
        grid_spec=pltpu.PrefetchScalarGridSpec(
            num_scalar_prefetch=1,
            grid=(2,),
            in_specs=[pl.BlockSpec((1, 1, rows, tokens), lambda j, *_: (0, j, 0, 0))] * steps
            + [
                pl.BlockSpec((steps, 1, rows, tokens), lambda j, *_: (0, j, 0, 0)),
                pl.BlockSpec((groups, tokens, hidden_here), lambda j, *_: (0, 0, j)),
            ],
            out_specs=pl.BlockSpec((1, 1, rows, hidden_here), lambda j, *_: (j, 0, 0, 0)),
        ),
        out_shape=jax.ShapeDtypeStruct((2, 1, rows, hidden_here), jnp.float32),
        compiler_params=pltpu.CompilerParams(vmem_limit_bytes=32 * 1024 * 1024),
        cost_estimate=pl.CostEstimate(
            flops=4 * rows * groups * tokens * hidden_here,
            bytes_accessed=4 * rows * groups * tokens + 16 * rows * hidden_here,
            transcendentals=0,
        ),
    )(position, *mine, theirs, both)


def body(cotangent, saved_inputs, up_weight, down_weight, block_owner):
    n_x = lax.axis_size("x")
    n_core = lax.axis_size("core")
    n_rep = n_x * n_core
    n_sh = lax.axis_size("sh")
    n_sl = lax.axis_size("sl")
    n_y = lax.axis_size("y")
    n_zh = lax.axis_size("zh")
    tokens, width = cotangent.shape
    block = up_weight.shape[0]
    hidden_here = up_weight.shape[1]

    up_full = lax.all_gather(up_weight, REP, axis=0, tiled=True)
    down_full = lax.all_gather(down_weight, REP, axis=1, tiled=True)

    pair = jnp.stack([saved_inputs.T, cotangent.T])
    spaced = spread(pair, ("sh", "zh"), n_sh * n_zh)
    column = lax.all_gather(spaced, "sl", axis=0, tiled=False)
    full = spread(column, "y", n_y)
    full = full.reshape(n_y, n_sl, n_sh, n_zh, 2, width, tokens)

    position = jnp.stack([lax.axis_index("x"), lax.axis_index("core")])
    inputs_flat, grads_flat, *messages = arrange(full, block_owner, position, n_x, n_core)
    messages = [piece.reshape(n_core, 2, block, tokens) for piece in messages]
    mine = [messages[0]] + [shift(messages[k], "x", k) for k in range(1, n_x)]

    inputs_flat = inputs_flat.reshape(n_rep * block, tokens)
    grads_flat = grads_flat.reshape(n_rep * block, tokens)
    pre_act = lax.dot_general(
        inputs_flat, up_full, (((0,), (0,)), ((), ())), preferred_element_type=jnp.float32
    )
    back_grad = lax.dot_general(
        grads_flat, down_full, (((0,), (1,)), ((), ())), preferred_element_type=jnp.float32
    )
    value, deriv = gelu_pair(pre_act)
    hidden = value.astype(jnp.bfloat16)
    dpre = (back_grad * deriv).astype(jnp.bfloat16)

    both = lax.all_gather(jnp.concatenate([dpre, hidden], axis=1), REP, axis=0, tiled=True)

    partial_grad = lax.dot_general(
        up_full, dpre, (((1,), (1,)), ((), ())), preferred_element_type=jnp.float32
    ).astype(jnp.bfloat16)
    partial_grad = partial_grad.reshape(n_sh, n_sl, n_y, n_zh, width, tokens)
    partial_grad = partial_grad.transpose(2, 1, 0, 3, 4, 5)
    parts = lax.all_to_all(partial_grad, "y", split_axis=0, concat_axis=0, tiled=True)
    parts = jnp.sum(parts.astype(jnp.float32), axis=0).astype(jnp.bfloat16)
    theirs = shift(collect(mine, parts), "core", 1)
    parts = lax.all_to_all(parts, "sl", split_axis=0, concat_axis=0, tiled=True)
    parts = jnp.sum(parts.astype(jnp.float32), axis=0).reshape(n_sh * n_zh, width, tokens)
    parts = lax.all_to_all(parts, ("sh", "zh"), split_axis=0, concat_axis=0, tiled=True)
    summed = jnp.sum(parts, axis=0).T
    input_grads = (cotangent.astype(jnp.float32) + summed).astype(jnp.bfloat16)

    weight_grads = block_grads(
        mine, theirs, both.reshape(n_rep, tokens, 2 * hidden_here), position, n_core
    )
    return (input_grads, weight_grads)


def solution(mesh):
    fine = Mesh(mesh.devices.reshape(4, 2, 2, 4, 4, 2), ("x", "core", "sh", "sl", "y", "zh"))
    in_specs = (
        P(REP, SHARD),
        P(REP, SHARD),
        P(REP, SHARD),
        P(SHARD, REP),
        P(),
    )
    out_specs = (P(REP, SHARD), P(None, REP, None, SHARD))
    return jax.shard_map(body, mesh=fine, in_specs=in_specs, out_specs=out_specs, check_vma=False)
```

```python
import math

import jax
import jax.numpy as jnp
from jax import lax
from jax.experimental import pallas as pl
from jax.experimental.pallas import tpu as pltpu
from jax.sharding import Mesh
from jax.sharding import PartitionSpec as P

GELU_SCALE = math.sqrt(2.0 / math.pi)
GELU_CUBIC = 0.044715

REP = ("x", "core")
SHARD = ("sh", "sl", "y", "zh")
VMEM = 60 * 1024 * 1024
SMALL = 24 * 1024 * 1024


def gelu_pair(values):
    tanh_part = jnp.tanh(GELU_SCALE * (values + GELU_CUBIC * values * values * values))
    value = 0.5 * values * (1.0 + tanh_part)
    deriv = 0.5 * (1.0 + tanh_part) + 0.5 * values * (1.0 - tanh_part * tanh_part) * GELU_SCALE * (
        1.0 + 3.0 * GELU_CUBIC * values * values
    )
    return value, deriv


def spread(block, axes, count):
    copies = lax.optimization_barrier(jnp.broadcast_to(block[None], (count,) + block.shape))
    return lax.all_to_all(copies, axes, split_axis=0, concat_axis=0, tiled=True)


def shift(block, axis, step):
    size = lax.axis_size(axis)
    return lax.ppermute(block, axis, [(i, (i + step) % size) for i in range(size)])


def end_of(position, e):
    return jnp.where(e == 0, position[1], 1 - position[1])


def arrange_kernel(owner, position, plain, here, ahead, across, behind, *refs):
    del owner, position
    flats, (own, up, down) = refs[:2], refs[2:]
    for j in range(2):

        @pl.when(pl.program_id(0) == j)
        def _(j=j):
            for b in range(plain.shape[1]):
                flats[j][b] = plain[:, b, 0, :, 0]

    own[0, 0] = here[:, 0, 0, :, 0]
    for e in range(2):

        @pl.when(pl.program_id(1) == e)
        def _(e=e):
            up[e, 0] = ahead[:, 0, 0, :, 0]
            down[e, 0] = behind[:, 0, 0, :, 0]
            (up, down)[e][2, 0] = across[:, 0, 0, :, 0]


def arrange(gathered, owner, position, n_x, n_core):
    n_y, n_sl, n_sh, n_zh, _, width, tokens = gathered.shape
    n_blocks = n_sl * n_sh
    piece = (n_y, 1, 1, n_zh, 1, width, tokens)

    def chosen_at(k):
        def index(j, e, owner, position):
            target = lax.rem(position[0] + k, n_x) * n_core + end_of(position, e)
            b = sum(jnp.where(owner[j, i] == target, i, 0) for i in range(n_blocks))
            return (0, lax.rem(b, n_sl), lax.div(b, n_sl), 0, j, 0, 0)

        return index

    out = (n_y, n_zh, width, tokens)
    return pl.pallas_call(
        arrange_kernel,
        grid_spec=pltpu.PrefetchScalarGridSpec(
            num_scalar_prefetch=2,
            grid=(2, n_sh),
            in_specs=[
                pl.BlockSpec(
                    (n_y, n_sl, 1, n_zh, 1, width, tokens), lambda j, h, *_: (0, 0, h, 0, j, 0, 0)
                )
            ]
            + [pl.BlockSpec(piece, chosen_at(k)) for k in range(n_x)],
            out_specs=[
                pl.BlockSpec(
                    (n_sl,) + out, lambda j, h, *_: (jnp.where(j == 0, h, n_sh - 1), 0, 0, 0, 0)
                ),
                pl.BlockSpec((n_sl,) + out, lambda j, h, *_: (jnp.where(j == 0, 0, h), 0, 0, 0, 0)),
            ]
            + [pl.BlockSpec((1, 1) + out, lambda j, e, *_: (e, j, 0, 0, 0, 0))]
            + [pl.BlockSpec((3, 1) + out, lambda j, e, *_: (0, j, 0, 0, 0, 0))] * 2,
        ),
        out_shape=[jax.ShapeDtypeStruct((n_blocks,) + out, gathered.dtype)] * 2
        + [jax.ShapeDtypeStruct((n_core, 2) + out, gathered.dtype)]
        + [jax.ShapeDtypeStruct((3, 2) + out, gathered.dtype)] * 2,
        compiler_params=pltpu.CompilerParams(vmem_limit_bytes=VMEM),
        cost_estimate=pl.CostEstimate(
            flops=0, bytes_accessed=8 * gathered.size, transcendentals=0
        ),
    )(owner, position, gathered, *([gathered] * n_x))


def collect_kernel(count, *refs):
    for k in range(count):
        refs[-1][k, 0] = refs[k][0, 0]


def collect(pieces, places, after):
    count = len(pieces)
    rows, tokens = pieces[0].shape[2:]
    return pl.pallas_call(
        lambda *refs: collect_kernel(count, *refs),
        grid=(2,),
        in_specs=[
            pl.BlockSpec((1, 1, rows, tokens), lambda j, place=place: (place, j, 0, 0))
            for place in places
        ]
        + [pl.BlockSpec(memory_space=pl.ANY)],
        out_specs=pl.BlockSpec((count, 1, rows, tokens), lambda j: (0, j, 0, 0)),
        out_shape=jax.ShapeDtypeStruct((count, 2, rows, tokens), pieces[0].dtype),
        compiler_params=pltpu.CompilerParams(vmem_limit_bytes=SMALL),
        cost_estimate=pl.CostEstimate(
            flops=0, bytes_accessed=8 * count * rows * tokens, transcendentals=0
        ),
    )(*pieces, after)


def middle_kernel(n_blocks, saved, grad, up, down, both, partial, pre, back, kept, turned):
    step = pl.program_id(0)

    @pl.when(step < n_blocks)
    def _():
        more = lax.dot_general(
            saved[...], up[...], (((0,), (0,)), ((), ())), preferred_element_type=jnp.float32
        )
        extra = jnp.dot(down[...], grad[...], preferred_element_type=jnp.float32)
        pre[...] = jnp.where(step == 0, 0.0, pre[...]) + more
        back[...] = jnp.where(step == 0, 0.0, back[...]) + extra
        kept[step] = up[...]

    @pl.when(step == n_blocks - 1)
    def _():
        value, deriv = gelu_pair(pre[...])
        dpre = (back[...].T * deriv).astype(jnp.bfloat16)
        columns = dpre.shape[1]
        both[:, :columns] = dpre
        both[:, columns:] = value.astype(jnp.bfloat16)
        turned[...] = dpre.T

    @pl.when(step >= n_blocks)
    def _():
        rows = jnp.dot(kept[step - n_blocks], turned[...], preferred_element_type=jnp.float32)
        shape = partial.shape
        partial[:, 0, 0] = rows.astype(jnp.bfloat16).reshape(shape[0], *shape[3:])


def middle(saved, grad, up_full, down_full, layout):
    n_y, n_sl, n_sh, n_zh, width = layout
    n_blocks = n_sl * n_sh
    features, tokens = saved.shape
    block = features // n_blocks
    hidden_here = up_full.shape[1]

    def first(i):
        return jnp.minimum(i, n_blocks - 1)

    def out_at(i):
        b = jnp.maximum(i - n_blocks, 0)
        return (0, lax.rem(b, n_sl), lax.div(b, n_sl), 0, 0, 0)

    return pl.pallas_call(
        lambda *refs: middle_kernel(n_blocks, *refs),
        grid=(2 * n_blocks,),
        in_specs=[
            pl.BlockSpec((block, tokens), lambda i: (first(i), 0)),
            pl.BlockSpec((block, tokens), lambda i: (first(i), 0)),
            pl.BlockSpec((block, hidden_here), lambda i: (first(i), 0)),
            pl.BlockSpec((hidden_here, block), lambda i: (0, first(i))),
        ],
        out_specs=[
            pl.BlockSpec((tokens, 2 * hidden_here), lambda i: (0, 0)),
            pl.BlockSpec((n_y, 1, 1, n_zh, width, tokens), out_at),
        ],
        out_shape=[
            jax.ShapeDtypeStruct((tokens, 2 * hidden_here), jnp.bfloat16),
            jax.ShapeDtypeStruct((n_y, n_sl, n_sh, n_zh, width, tokens), jnp.bfloat16),
        ],
        scratch_shapes=[
            pltpu.VMEM((tokens, hidden_here), jnp.float32),
            pltpu.VMEM((hidden_here, tokens), jnp.float32),
            pltpu.VMEM((n_blocks, block, hidden_here), jnp.bfloat16),
            pltpu.VMEM((hidden_here, tokens), jnp.bfloat16),
        ],
        compiler_params=pltpu.CompilerParams(vmem_limit_bytes=VMEM),
        cost_estimate=pl.CostEstimate(
            flops=6 * tokens * features * hidden_here,
            bytes_accessed=4 * features * hidden_here + 6 * features * tokens,
            transcendentals=tokens * hidden_here,
        ),
    )(saved, grad, up_full, down_full)


def grads_kernel(steps, n_core, position, *refs):
    mine, (theirs, both, out) = refs[:steps], refs[steps:]
    total = None
    for k in range(steps):
        row = lax.rem(position[0] + (steps - k), steps) * n_core
        left = jnp.concatenate([mine[k][0, 0], theirs[k, 0]], axis=1)
        right = jnp.concatenate([both[row + position[1]], both[row + 1 - position[1]]], axis=0)
        term = jnp.dot(left, right, preferred_element_type=jnp.float32)
        total = term if total is None else total + term
    out[0, 0] = total


def block_grads(mine, theirs, both, position, n_core):
    steps = len(mine)
    rows, tokens = mine[0].shape[2:]
    groups, _, columns = both.shape
    hidden_here = columns // 2
    return pl.pallas_call(
        lambda *refs: grads_kernel(steps, n_core, *refs),
        grid_spec=pltpu.PrefetchScalarGridSpec(
            num_scalar_prefetch=1,
            grid=(2,),
            in_specs=[pl.BlockSpec((1, 1, rows, tokens), lambda j, *_: (0, j, 0, 0))] * steps
            + [
                pl.BlockSpec((steps, 1, rows, tokens), lambda j, *_: (0, j, 0, 0)),
                pl.BlockSpec((groups, tokens, hidden_here), lambda j, *_: (0, 0, j)),
            ],
            out_specs=pl.BlockSpec((1, 1, rows, hidden_here), lambda j, *_: (j, 0, 0, 0)),
        ),
        out_shape=jax.ShapeDtypeStruct((2, 1, rows, hidden_here), jnp.float32),
        compiler_params=pltpu.CompilerParams(vmem_limit_bytes=SMALL),
        cost_estimate=pl.CostEstimate(
            flops=4 * rows * groups * tokens * hidden_here,
            bytes_accessed=4 * rows * groups * tokens + 16 * rows * hidden_here,
            transcendentals=0,
        ),
    )(position, *mine, theirs, both)


def body(cotangent, saved_inputs, up_weight, down_weight, block_owner):
    n_x = lax.axis_size("x")
    n_core = lax.axis_size("core")
    n_rep = n_x * n_core
    n_sh = lax.axis_size("sh")
    n_sl = lax.axis_size("sl")
    n_y = lax.axis_size("y")
    n_zh = lax.axis_size("zh")
    tokens, width = cotangent.shape
    block = up_weight.shape[0]

    up_full = lax.all_gather(up_weight, REP, axis=0, tiled=True)
    down_full = lax.all_gather(down_weight, REP, axis=1, tiled=True)

    pair = jnp.stack([saved_inputs.T, cotangent.T])
    spaced = spread(pair, ("sh", "zh"), n_sh * n_zh)
    column = lax.all_gather(spaced, "sl", axis=0, tiled=False)
    full = spread(column, "y", n_y)
    full = full.reshape(n_y, n_sl, n_sh, n_zh, 2, width, tokens)

    position = jnp.stack([lax.axis_index("x"), lax.axis_index("core")])
    inputs_flat, grads_flat, own, up, down = arrange(full, block_owner, position, n_x, n_core)
    own, up, down = (
        piece.reshape(piece.shape[0], 2, block, tokens) for piece in (own, up, down)
    )
    below = shift(up, "x", 1)
    above = shift(down, "x", n_x - 1)

    both, partial_grad = middle(
        inputs_flat.reshape(n_rep * block, tokens),
        grads_flat.reshape(n_rep * block, tokens),
        up_full,
        down_full,
        (n_y, n_sl, n_sh, n_zh, width),
    )
    both = lax.all_gather(both, REP, axis=0, tiled=True)

    parts = lax.all_to_all(partial_grad, "y", split_axis=0, concat_axis=0, tiled=True)
    parts = jnp.sum(parts.astype(jnp.float32), axis=0).astype(jnp.bfloat16)
    across = shift(collect([below], [2], parts), "x", 1)
    return_across = shift(collect([above], [2], parts), "x", n_x - 1)
    parts = lax.all_to_all(parts, "sl", split_axis=0, concat_axis=0, tiled=True)
    parts = jnp.sum(parts.astype(jnp.float32), axis=0).reshape(n_sh * n_zh, width, tokens)
    theirs = collect([own, below, return_across, above], [1, 1, 0, 1], parts)
    theirs = shift(theirs, "core", 1)
    parts = lax.all_to_all(parts, ("sh", "zh"), split_axis=0, concat_axis=0, tiled=True)
    summed = jnp.sum(parts, axis=0).T
    input_grads = (cotangent.astype(jnp.float32) + summed).astype(jnp.bfloat16)

    mine = [own, below, across, above]
    weight_grads = block_grads(
        mine, theirs, both.reshape(n_rep, tokens, -1), position, n_core
    )
    return (input_grads, weight_grads)


def solution(mesh):
    fine = Mesh(mesh.devices.reshape(4, 2, 2, 4, 4, 2), ("x", "core", "sh", "sl", "y", "zh"))
    in_specs = (
        P(REP, SHARD),
        P(REP, SHARD),
        P(REP, SHARD),
        P(SHARD, REP),
        P(),
    )
    out_specs = (P(REP, SHARD), P(None, REP, None, SHARD))
    return jax.shard_map(body, mesh=fine, in_specs=in_specs, out_specs=out_specs, check_vma=False)
```

```python
import math

import jax
import jax.numpy as jnp
from jax import lax
from jax.experimental import pallas as pl
from jax.experimental.pallas import tpu as pltpu
from jax.sharding import Mesh
from jax.sharding import PartitionSpec as P

GELU_SCALE = math.sqrt(2.0 / math.pi)
GELU_CUBIC = 0.044715

REP = ("x", "core")
SHARD = ("sh", "sl", "y", "zh")
SMALL = 24 * 1024 * 1024
LARGE = 60 * 1024 * 1024


def gelu_pair(values):
    tanh_part = jnp.tanh(GELU_SCALE * (values + GELU_CUBIC * values * values * values))
    value = 0.5 * values * (1.0 + tanh_part)
    deriv = 0.5 * (1.0 + tanh_part) + 0.5 * values * (1.0 - tanh_part * tanh_part) * GELU_SCALE * (
        1.0 + 3.0 * GELU_CUBIC * values * values
    )
    return value, deriv


def spread(block, axes, count):
    copies = lax.optimization_barrier(jnp.broadcast_to(block[None], (count,) + block.shape))
    return lax.all_to_all(copies, axes, split_axis=0, concat_axis=0, tiled=True)


def arrange_kernel(owner, plain, *refs):
    del owner
    count = plain.shape[1]
    chosen, (first, second, message) = refs[:count], refs[-3:]
    for j, flat in enumerate((first, second)):

        @pl.when(pl.program_id(0) == j)
        def _(flat=flat):
            for b in range(count):
                flat[b] = plain[:, b, 0, :, 0]

    for k in range(count):
        message[k, 0] = chosen[k][:, 0, 0, :, 0]


def arrange(gathered, owner, after):
    n_y, n_sl, n_sh, n_zh, _, width, tokens = gathered.shape
    n_blocks = n_sl * n_sh
    piece = (n_y, 1, 1, n_zh, 1, width, tokens)

    def chosen_at(k):
        def index(j, h, owner):
            target = h * n_sl + k
            b = sum(jnp.where(owner[j, i] == target, i, 0) for i in range(n_blocks))
            return (0, lax.rem(b, n_sl), lax.div(b, n_sl), 0, j, 0, 0)

        return index

    out = (n_y, n_zh, width, tokens)
    return pl.pallas_call(
        arrange_kernel,
        grid_spec=pltpu.PrefetchScalarGridSpec(
            num_scalar_prefetch=1,
            grid=(2, n_sh),
            in_specs=[
                pl.BlockSpec(
                    (n_y, n_sl, 1, n_zh, 1, width, tokens), lambda j, h, _: (0, 0, h, 0, j, 0, 0)
                )
            ]
            + [pl.BlockSpec(piece, chosen_at(k)) for k in range(n_sl)]
            + [pl.BlockSpec(memory_space=pl.ANY)] * len(after),
            out_specs=[
                pl.BlockSpec(
                    (n_sl,) + out, lambda j, h, _: (jnp.where(j == 0, h, n_sh - 1), 0, 0, 0, 0)
                ),
                pl.BlockSpec((n_sl,) + out, lambda j, h, _: (jnp.where(j == 0, 0, h), 0, 0, 0, 0)),
                pl.BlockSpec((n_sl, 1) + out, lambda j, h, _: (h, j, 0, 0, 0, 0)),
            ],
        ),
        out_shape=[jax.ShapeDtypeStruct((n_blocks,) + out, gathered.dtype)] * 2
        + [jax.ShapeDtypeStruct((n_blocks, 2) + out, gathered.dtype)],
        compiler_params=pltpu.CompilerParams(vmem_limit_bytes=SMALL),
        cost_estimate=pl.CostEstimate(
            flops=0, bytes_accessed=8 * gathered.size, transcendentals=0
        ),
    )(owner, gathered, *([gathered] * n_sl), *after)


def share_kernel(mine, up, dpre, *refs):
    outs, rows = refs[:-1], refs[-1]
    n_y = rows.shape[0]
    product = lax.dot_general(
        up[...], dpre[...], (((1,), (1,)), ((), ())), preferred_element_type=jnp.float32
    )
    rows[...] = product.astype(rows.dtype).reshape(rows.shape)
    for k in range(n_y):
        outs[k][0, 0] = rows[lax.rem(mine[0] + k, n_y)]


def share(up_full, dpre, mine, layout):
    n_y, n_sl, n_sh, n_zh, width = layout
    n_blocks = n_sl * n_sh
    tokens, hidden_here = dpre.shape
    block = up_full.shape[0] // n_blocks
    return pl.pallas_call(
        share_kernel,
        grid_spec=pltpu.PrefetchScalarGridSpec(
            num_scalar_prefetch=1,
            grid=(n_blocks,),
            in_specs=[
                pl.BlockSpec((block, hidden_here), lambda i, _: (i, 0)),
                pl.BlockSpec((tokens, hidden_here), lambda i, _: (0, 0)),
            ],
            out_specs=[
                pl.BlockSpec(
                    (1, 1, n_zh, width, tokens),
                    lambda i, _: (lax.rem(i, n_sl), lax.div(i, n_sl), 0, 0, 0),
                )
            ]
            * n_y,
            scratch_shapes=[pltpu.VMEM((n_y, n_zh, width, tokens), jnp.bfloat16)],
        ),
        out_shape=[jax.ShapeDtypeStruct((n_sl, n_sh, n_zh, width, tokens), jnp.bfloat16)] * n_y,
        compiler_params=pltpu.CompilerParams(vmem_limit_bytes=LARGE),
        cost_estimate=pl.CostEstimate(
            flops=2 * tokens * hidden_here * block * n_blocks,
            bytes_accessed=2 * block * n_blocks * (hidden_here + tokens),
            transcendentals=0,
        ),
    )(mine, up_full, dpre)


def fold_kernel(count, mine, *refs):
    terms = refs[:count]
    size = terms[0].shape[0]
    outs = refs[-size:]
    for k in range(size):
        at = lax.rem(mine[0] + k, size)
        total = terms[0][at].astype(jnp.float32)
        for term in terms[1:]:
            total = total + term[at].astype(jnp.float32)
        outs[k][...] = total.astype(outs[k].dtype)


def fold(terms, mine, kind, after=()):
    size, *rest = terms[0].shape
    return pl.pallas_call(
        lambda *refs: fold_kernel(len(terms), *refs),
        grid_spec=pltpu.PrefetchScalarGridSpec(
            num_scalar_prefetch=1,
            grid=(1,),
            in_specs=[pl.BlockSpec((size, *rest), lambda i, _: (0,) * (len(rest) + 1))] * len(terms)
            + [pl.BlockSpec(memory_space=pl.ANY)] * len(after),
            out_specs=[pl.BlockSpec(tuple(rest), lambda i, _: (0,) * len(rest))] * size,
        ),
        out_shape=[jax.ShapeDtypeStruct(tuple(rest), kind)] * size,
        compiler_params=pltpu.CompilerParams(vmem_limit_bytes=SMALL),
    )(mine, *terms, *after)


def grads_kernel(pieces, both, out):
    total = None
    for r in range(0, pieces.shape[0], 2):
        left = jnp.concatenate([pieces[r, 0], pieces[r + 1, 0]], axis=1)
        right = jnp.concatenate([both[r], both[r + 1]], axis=0)
        term = jnp.dot(left, right, preferred_element_type=jnp.float32)
        total = term if total is None else total + term
    out[0, 0] = total


def block_grads(pieces, both):
    groups, _, rows, tokens = pieces.shape
    hidden_here = both.shape[2] // 2
    return pl.pallas_call(
        grads_kernel,
        grid=(2,),
        in_specs=[
            pl.BlockSpec((groups, 1, rows, tokens), lambda j: (0, j, 0, 0)),
            pl.BlockSpec((groups, tokens, hidden_here), lambda j: (0, 0, j)),
        ],
        out_specs=pl.BlockSpec((1, 1, rows, hidden_here), lambda j: (j, 0, 0, 0)),
        out_shape=jax.ShapeDtypeStruct((2, 1, rows, hidden_here), jnp.float32),
        compiler_params=pltpu.CompilerParams(vmem_limit_bytes=SMALL),
        cost_estimate=pl.CostEstimate(
            flops=4 * rows * groups * tokens * hidden_here,
            bytes_accessed=4 * rows * groups * tokens + 16 * rows * hidden_here,
            transcendentals=0,
        ),
    )(pieces, both)


def trade(steps, axes):
    size = lax.axis_size(axes)
    return [steps[0]] + [
        lax.ppermute(steps[k], axes, [(i, (i + k) % size) for i in range(size)])
        for k in range(1, size)
    ]


def place(axes):
    return jnp.reshape(lax.axis_index(axes), (1,))


def body(cotangent, saved_inputs, up_weight, down_weight, block_owner):
    n_x = lax.axis_size("x")
    n_core = lax.axis_size("core")
    n_rep = n_x * n_core
    n_sh = lax.axis_size("sh")
    n_sl = lax.axis_size("sl")
    n_y = lax.axis_size("y")
    n_zh = lax.axis_size("zh")
    tokens, width = cotangent.shape
    block = up_weight.shape[0]

    up_full = lax.all_gather(up_weight, REP, axis=0, tiled=True)
    down_full = lax.all_gather(down_weight, REP, axis=1, tiled=True)

    pair = jnp.stack([saved_inputs.T, cotangent.T])
    spaced = spread(pair, ("sh", "zh"), n_sh * n_zh)
    column = lax.all_gather(spaced, "sl", axis=0, tiled=False)
    full = spread(column, "y", n_y)
    full = full.reshape(n_y, n_sl, n_sh, n_zh, 2, width, tokens)

    inputs_flat, grads_flat, message = arrange(
        full, block_owner, (up_full[:16, :128], down_full[:16, :128])
    )
    message = message.reshape(n_rep, 2, block, tokens)
    owned = lax.all_to_all(message, REP, split_axis=0, concat_axis=0, tiled=True)

    inputs_flat = inputs_flat.reshape(n_rep * block, tokens)
    grads_flat = grads_flat.reshape(n_rep * block, tokens)
    pre_act = lax.dot_general(
        inputs_flat, up_full, (((0,), (0,)), ((), ())), preferred_element_type=jnp.float32
    )
    back_grad = lax.dot_general(
        grads_flat, down_full, (((0,), (1,)), ((), ())), preferred_element_type=jnp.float32
    )
    value, deriv = gelu_pair(pre_act)
    hidden = value.astype(jnp.bfloat16)
    dpre = (back_grad * deriv).astype(jnp.bfloat16)

    both = lax.all_gather(jnp.concatenate([dpre, hidden], axis=1), REP, axis=0, tiled=True)

    layout = (n_y, n_sl, n_sh, n_zh, width)
    parts = trade(share(up_full, dpre, place("y"), layout), "y")
    parts = trade(fold(parts, place("sl"), jnp.bfloat16), "sl")
    parts = [p.reshape(n_sh * n_zh, width, tokens) for p in parts]
    parts = trade(fold(parts, place(("sh", "zh")), jnp.float32, (owned,)), ("sh", "zh"))
    summed = sum(parts[1:], parts[0]).T
    input_grads = (cotangent.astype(jnp.float32) + summed).astype(jnp.bfloat16)

    weight_grads = block_grads(owned, both.reshape(n_rep, tokens, -1))
    return (input_grads, weight_grads)


def solution(mesh):
    fine = Mesh(mesh.devices.reshape(4, 2, 2, 4, 4, 2), ("x", "core", "sh", "sl", "y", "zh"))
    in_specs = (
        P(REP, SHARD),
        P(REP, SHARD),
        P(REP, SHARD),
        P(SHARD, REP),
        P(),
    )
    out_specs = (P(REP, SHARD), P(None, REP, None, SHARD))
    return jax.shard_map(body, mesh=fine, in_specs=in_specs, out_specs=out_specs, check_vma=False)
```

```python
import math

import jax
import jax.numpy as jnp
from jax import lax
from jax.experimental import pallas as pl
from jax.experimental.pallas import tpu as pltpu
from jax.sharding import Mesh
from jax.sharding import PartitionSpec as P

GELU_SCALE = math.sqrt(2.0 / math.pi)
GELU_CUBIC = 0.044715

REP = ("x", "core")
SHARD = ("sh", "sl", "y", "zh")
SMALL = 24 * 1024 * 1024


def gelu_pair(values):
    tanh_part = jnp.tanh(GELU_SCALE * (values + GELU_CUBIC * values * values * values))
    value = 0.5 * values * (1.0 + tanh_part)
    deriv = 0.5 * (1.0 + tanh_part) + 0.5 * values * (1.0 - tanh_part * tanh_part) * GELU_SCALE * (
        1.0 + 3.0 * GELU_CUBIC * values * values
    )
    return value, deriv


def spread(block, axes, count):
    copies = lax.optimization_barrier(jnp.broadcast_to(block[None], (count,) + block.shape))
    return lax.all_to_all(copies, axes, split_axis=0, concat_axis=0, tiled=True)


def arrange_kernel(owner, plain, *refs):
    del owner
    count = plain.shape[1]
    chosen, (first, second, message) = refs[:count], refs[-3:]
    for j, flat in enumerate((first, second)):

        @pl.when(pl.program_id(0) == j)
        def _(flat=flat):
            for b in range(count):
                flat[b] = plain[:, b, 0, :, 0]

    for k in range(count):
        message[k, 0] = chosen[k][:, 0, 0, :, 0]


def arrange(gathered, owner, after):
    n_y, n_sl, n_sh, n_zh, _, width, tokens = gathered.shape
    n_blocks = n_sl * n_sh
    piece = (n_y, 1, 1, n_zh, 1, width, tokens)

    def chosen_at(k):
        def index(j, h, owner):
            target = h * n_sl + k
            b = sum(jnp.where(owner[j, i] == target, i, 0) for i in range(n_blocks))
            return (0, lax.rem(b, n_sl), lax.div(b, n_sl), 0, j, 0, 0)

        return index

    out = (n_y, n_zh, width, tokens)
    return pl.pallas_call(
        arrange_kernel,
        grid_spec=pltpu.PrefetchScalarGridSpec(
            num_scalar_prefetch=1,
            grid=(2, n_sh),
            in_specs=[
                pl.BlockSpec(
                    (n_y, n_sl, 1, n_zh, 1, width, tokens), lambda j, h, _: (0, 0, h, 0, j, 0, 0)
                )
            ]
            + [pl.BlockSpec(piece, chosen_at(k)) for k in range(n_sl)]
            + [pl.BlockSpec(memory_space=pl.ANY)] * len(after),
            out_specs=[
                pl.BlockSpec(
                    (n_sl,) + out, lambda j, h, _: (jnp.where(j == 0, h, n_sh - 1), 0, 0, 0, 0)
                ),
                pl.BlockSpec((n_sl,) + out, lambda j, h, _: (jnp.where(j == 0, 0, h), 0, 0, 0, 0)),
                pl.BlockSpec((n_sl, 1) + out, lambda j, h, _: (h, j, 0, 0, 0, 0)),
            ],
        ),
        out_shape=[jax.ShapeDtypeStruct((n_blocks,) + out, gathered.dtype)] * 2
        + [jax.ShapeDtypeStruct((n_blocks, 2) + out, gathered.dtype)],
        compiler_params=pltpu.CompilerParams(vmem_limit_bytes=SMALL),
        cost_estimate=pl.CostEstimate(
            flops=0, bytes_accessed=8 * gathered.size, transcendentals=0
        ),
    )(owner, gathered, *([gathered] * n_sl), *after)


def cut_kernel(mine, *refs):
    del mine
    count = len(refs) // 2
    for k in range(count):
        refs[count + k][...] = refs[k][:, 0]


def cut(rows, mine):
    n_blocks, n_y, *rest = rows.shape
    zeros = (0,) * len(rest)
    return pl.pallas_call(
        cut_kernel,
        grid_spec=pltpu.PrefetchScalarGridSpec(
            num_scalar_prefetch=1,
            grid=(2,),
            in_specs=[
                pl.BlockSpec(
                    (n_blocks // 2, 1, *rest),
                    lambda i, mine, k=k: (i, lax.rem(mine[0] + k, n_y), *zeros),
                )
                for k in range(n_y)
            ],
            out_specs=[pl.BlockSpec((n_blocks // 2, *rest), lambda i, _: (i, *zeros))] * n_y,
        ),
        out_shape=[jax.ShapeDtypeStruct((n_blocks, *rest), rows.dtype)] * n_y,
        compiler_params=pltpu.CompilerParams(vmem_limit_bytes=SMALL),
    )(mine, *([rows] * n_y))


def total_kernel(count, *refs):
    total = refs[0][...].astype(jnp.float32)
    for term in refs[1:count]:
        total = total + term[...].astype(jnp.float32)
    refs[-1][...] = total.astype(refs[-1].dtype)


def total(terms, after):
    shape = terms[0].shape
    half = (shape[0] // 2, *shape[1:])
    spec = pl.BlockSpec(half, lambda i: (i,) + (0,) * (len(shape) - 1))
    return pl.pallas_call(
        lambda *refs: total_kernel(len(terms), *refs),
        grid=(2,),
        in_specs=[spec] * len(terms) + [pl.BlockSpec(memory_space=pl.ANY)],
        out_specs=spec,
        out_shape=jax.ShapeDtypeStruct(shape, terms[0].dtype),
        compiler_params=pltpu.CompilerParams(vmem_limit_bytes=SMALL),
    )(*terms, after)


def grads_kernel(pieces, both, out):
    total = None
    for r in range(0, pieces.shape[0], 2):
        left = jnp.concatenate([pieces[r, 0], pieces[r + 1, 0]], axis=1)
        right = jnp.concatenate([both[r], both[r + 1]], axis=0)
        term = jnp.dot(left, right, preferred_element_type=jnp.float32)
        total = term if total is None else total + term
    out[0, 0] = total


def block_grads(pieces, both):
    groups, _, rows, tokens = pieces.shape
    hidden_here = both.shape[2] // 2
    return pl.pallas_call(
        grads_kernel,
        grid=(2,),
        in_specs=[
            pl.BlockSpec((groups, 1, rows, tokens), lambda j: (0, j, 0, 0)),
            pl.BlockSpec((groups, tokens, hidden_here), lambda j: (0, 0, j)),
        ],
        out_specs=pl.BlockSpec((1, 1, rows, hidden_here), lambda j: (j, 0, 0, 0)),
        out_shape=jax.ShapeDtypeStruct((2, 1, rows, hidden_here), jnp.float32),
        compiler_params=pltpu.CompilerParams(vmem_limit_bytes=SMALL),
        cost_estimate=pl.CostEstimate(
            flops=4 * rows * groups * tokens * hidden_here,
            bytes_accessed=4 * rows * groups * tokens + 16 * rows * hidden_here,
            transcendentals=0,
        ),
    )(pieces, both)


def trade(steps, axes):
    size = lax.axis_size(axes)
    return [steps[0]] + [
        lax.ppermute(steps[k], axes, [(i, (i + k) % size) for i in range(size)])
        for k in range(1, size)
    ]


def place(axes):
    return jnp.reshape(lax.axis_index(axes), (1,))


def body(cotangent, saved_inputs, up_weight, down_weight, block_owner):
    n_x = lax.axis_size("x")
    n_core = lax.axis_size("core")
    n_rep = n_x * n_core
    n_sh = lax.axis_size("sh")
    n_sl = lax.axis_size("sl")
    n_y = lax.axis_size("y")
    n_zh = lax.axis_size("zh")
    tokens, width = cotangent.shape
    block = up_weight.shape[0]

    up_full = lax.all_gather(up_weight, REP, axis=0, tiled=True)
    down_full = lax.all_gather(down_weight, REP, axis=1, tiled=True)

    pair = jnp.stack([saved_inputs.T, cotangent.T])
    spaced = spread(pair, ("sh", "zh"), n_sh * n_zh)
    column = lax.all_gather(spaced, "sl", axis=0, tiled=False)
    full = spread(column, "y", n_y)
    full = full.reshape(n_y, n_sl, n_sh, n_zh, 2, width, tokens)

    inputs_flat, grads_flat, message = arrange(
        full, block_owner, (up_full[:16, :128], down_full[:16, :128])
    )
    message = message.reshape(n_rep, 2, block, tokens)
    owned = lax.all_to_all(message, REP, split_axis=0, concat_axis=0, tiled=True)

    inputs_flat = inputs_flat.reshape(n_rep * block, tokens)
    grads_flat = grads_flat.reshape(n_rep * block, tokens)
    pre_act = lax.dot_general(
        inputs_flat, up_full, (((0,), (0,)), ((), ())), preferred_element_type=jnp.float32
    )
    back_grad = lax.dot_general(
        grads_flat, down_full, (((0,), (1,)), ((), ())), preferred_element_type=jnp.float32
    )
    value, deriv = gelu_pair(pre_act)
    hidden = value.astype(jnp.bfloat16)
    dpre = (back_grad * deriv).astype(jnp.bfloat16)

    both = lax.all_gather(jnp.concatenate([dpre, hidden], axis=1), REP, axis=0, tiled=True)

    partial_grad = lax.dot_general(
        up_full, dpre, (((1,), (1,)), ((), ())), preferred_element_type=jnp.float32
    ).astype(jnp.bfloat16)
    parts = cut(partial_grad.reshape(n_rep, n_y, n_zh, width, tokens), place("y"))
    parts = total(trade(parts, "y"), owned).reshape(n_rep * n_zh, width, tokens)
    parts = lax.all_to_all(parts, ("sh", "sl", "zh"), split_axis=0, concat_axis=0, tiled=True)
    summed = jnp.sum(parts.astype(jnp.float32), axis=0).T
    input_grads = (cotangent.astype(jnp.float32) + summed).astype(jnp.bfloat16)

    weight_grads = block_grads(owned, both.reshape(n_rep, tokens, -1))
    return (input_grads, weight_grads)


def solution(mesh):
    fine = Mesh(mesh.devices.reshape(4, 2, 2, 4, 4, 2), ("x", "core", "sh", "sl", "y", "zh"))
    in_specs = (
        P(REP, SHARD),
        P(REP, SHARD),
        P(REP, SHARD),
        P(SHARD, REP),
        P(),
    )
    out_specs = (P(REP, SHARD), P(None, REP, None, SHARD))
    return jax.shard_map(body, mesh=fine, in_specs=in_specs, out_specs=out_specs, check_vma=False)
```

```python
import math

import jax
import jax.numpy as jnp
from jax import lax
from jax.experimental import pallas as pl
from jax.experimental.pallas import tpu as pltpu
from jax.sharding import Mesh
from jax.sharding import PartitionSpec as P

GELU_SCALE = math.sqrt(2.0 / math.pi)
GELU_CUBIC = 0.044715

REP = ("x", "core")
SHARD = ("sh", "sl", "y", "zh")
SMALL = 24 * 1024 * 1024


def gelu_pair(values):
    tanh_part = jnp.tanh(GELU_SCALE * (values + GELU_CUBIC * values * values * values))
    value = 0.5 * values * (1.0 + tanh_part)
    deriv = 0.5 * (1.0 + tanh_part) + 0.5 * values * (1.0 - tanh_part * tanh_part) * GELU_SCALE * (
        1.0 + 3.0 * GELU_CUBIC * values * values
    )
    return value, deriv


def spread(block, axes, count):
    copies = lax.optimization_barrier(jnp.broadcast_to(block[None], (count,) + block.shape))
    return lax.all_to_all(copies, axes, split_axis=0, concat_axis=0, tiled=True)


def arrange_kernel(owner, plain, *refs):
    del owner
    count = plain.shape[1]
    chosen, (first, second, message) = refs[:count], refs[-3:]
    for j, flat in enumerate((first, second)):

        @pl.when(pl.program_id(0) == j)
        def _(flat=flat):
            for b in range(count):
                flat[b] = plain[:, b, 0, :, 0]

    for k in range(count):
        message[k, 0] = chosen[k][:, 0, 0, :, 0]


def arrange(gathered, owner, after):
    n_y, n_sl, n_sh, n_zh, _, width, tokens = gathered.shape
    n_blocks = n_sl * n_sh
    piece = (n_y, 1, 1, n_zh, 1, width, tokens)

    def chosen_at(k):
        def index(j, h, owner):
            target = h * n_sl + k
            b = sum(jnp.where(owner[j, i] == target, i, 0) for i in range(n_blocks))
            return (0, lax.rem(b, n_sl), lax.div(b, n_sl), 0, j, 0, 0)

        return index

    out = (n_y, n_zh, width, tokens)
    return pl.pallas_call(
        arrange_kernel,
        grid_spec=pltpu.PrefetchScalarGridSpec(
            num_scalar_prefetch=1,
            grid=(2, n_sh),
            in_specs=[
                pl.BlockSpec(
                    (n_y, n_sl, 1, n_zh, 1, width, tokens), lambda j, h, _: (0, 0, h, 0, j, 0, 0)
                )
            ]
            + [pl.BlockSpec(piece, chosen_at(k)) for k in range(n_sl)]
            + [pl.BlockSpec(memory_space=pl.ANY)] * len(after),
            out_specs=[
                pl.BlockSpec(
                    (n_sl,) + out, lambda j, h, _: (jnp.where(j == 0, h, n_sh - 1), 0, 0, 0, 0)
                ),
                pl.BlockSpec((n_sl,) + out, lambda j, h, _: (jnp.where(j == 0, 0, h), 0, 0, 0, 0)),
                pl.BlockSpec((n_sl, 1) + out, lambda j, h, _: (h, j, 0, 0, 0, 0)),
            ],
        ),
        out_shape=[jax.ShapeDtypeStruct((n_blocks,) + out, gathered.dtype)] * 2
        + [jax.ShapeDtypeStruct((n_blocks, 2) + out, gathered.dtype)],
        compiler_params=pltpu.CompilerParams(vmem_limit_bytes=SMALL),
        cost_estimate=pl.CostEstimate(
            flops=0, bytes_accessed=8 * gathered.size, transcendentals=0
        ),
    )(owner, gathered, *([gathered] * n_sl), *after)


def cut_kernel(mine, *refs):
    del mine
    count = len(refs) // 2
    for k in range(count):
        refs[count + k][:, 0] = refs[k][:, 0]


def cut(rows, mine, n_sh):
    n_blocks, n_y, *rest = rows.shape
    n_sl = n_blocks // n_sh
    zeros = (0,) * len(rest)
    return pl.pallas_call(
        cut_kernel,
        grid_spec=pltpu.PrefetchScalarGridSpec(
            num_scalar_prefetch=1,
            grid=(n_sh,),
            in_specs=[
                pl.BlockSpec(
                    (n_sl, 1, *rest), lambda i, mine, k=k: (i, lax.rem(mine[0] + k, n_y), *zeros)
                )
                for k in range(n_y)
            ],
            out_specs=[pl.BlockSpec((n_sl, 1, *rest), lambda i, _: (0, i, *zeros))] * n_y,
        ),
        out_shape=[jax.ShapeDtypeStruct((n_sl, n_sh, *rest), rows.dtype)] * n_y,
        compiler_params=pltpu.CompilerParams(vmem_limit_bytes=SMALL),
    )(mine, *([rows] * n_y))


def fold_kernel(count, mine, *refs):
    terms, outs = refs[:count], refs[count:]
    for k in range(len(outs)):
        at = lax.rem(mine[0] + k, len(outs))
        total = terms[0][at].astype(jnp.float32)
        for term in terms[1:]:
            total = total + term[at].astype(jnp.float32)
        outs[k][...] = total.astype(outs[k].dtype)


def fold(terms, mine):
    size, *rest = terms[0].shape
    return pl.pallas_call(
        lambda *refs: fold_kernel(len(terms), *refs),
        grid_spec=pltpu.PrefetchScalarGridSpec(
            num_scalar_prefetch=1,
            grid=(1,),
            in_specs=[pl.BlockSpec((size, *rest), lambda i, _: (0,) * (len(rest) + 1))] * len(terms),
            out_specs=[pl.BlockSpec(tuple(rest), lambda i, _: (0,) * len(rest))] * size,
        ),
        out_shape=[jax.ShapeDtypeStruct(tuple(rest), terms[0].dtype)] * size,
        compiler_params=pltpu.CompilerParams(vmem_limit_bytes=SMALL),
    )(mine, *terms)


def total_kernel(count, *refs):
    total = refs[0][...].astype(jnp.float32)
    for term in refs[1:count]:
        total = total + term[...].astype(jnp.float32)
    refs[-1][...] = total.astype(refs[-1].dtype)


def total(terms, after):
    shape = terms[0].shape
    half = (shape[0] // 2, *shape[1:])
    spec = pl.BlockSpec(half, lambda i: (i,) + (0,) * (len(shape) - 1))
    return pl.pallas_call(
        lambda *refs: total_kernel(len(terms), *refs),
        grid=(2,),
        in_specs=[spec] * len(terms) + [pl.BlockSpec(memory_space=pl.ANY)],
        out_specs=spec,
        out_shape=jax.ShapeDtypeStruct(shape, terms[0].dtype),
        compiler_params=pltpu.CompilerParams(vmem_limit_bytes=SMALL),
    )(*terms, after)


def grads_kernel(pieces, both, out):
    total = None
    for r in range(0, pieces.shape[0], 2):
        left = jnp.concatenate([pieces[r, 0], pieces[r + 1, 0]], axis=1)
        right = jnp.concatenate([both[r], both[r + 1]], axis=0)
        term = jnp.dot(left, right, preferred_element_type=jnp.float32)
        total = term if total is None else total + term
    out[0, 0] = total


def block_grads(pieces, both):
    groups, _, rows, tokens = pieces.shape
    hidden_here = both.shape[2] // 2
    return pl.pallas_call(
        grads_kernel,
        grid=(2,),
        in_specs=[
            pl.BlockSpec((groups, 1, rows, tokens), lambda j: (0, j, 0, 0)),
            pl.BlockSpec((groups, tokens, hidden_here), lambda j: (0, 0, j)),
        ],
        out_specs=pl.BlockSpec((1, 1, rows, hidden_here), lambda j: (j, 0, 0, 0)),
        out_shape=jax.ShapeDtypeStruct((2, 1, rows, hidden_here), jnp.float32),
        compiler_params=pltpu.CompilerParams(vmem_limit_bytes=SMALL),
        cost_estimate=pl.CostEstimate(
            flops=4 * rows * groups * tokens * hidden_here,
            bytes_accessed=4 * rows * groups * tokens + 16 * rows * hidden_here,
            transcendentals=0,
        ),
    )(pieces, both)


def trade(steps, axes):
    size = lax.axis_size(axes)
    return [steps[0]] + [
        lax.ppermute(steps[k], axes, [(i, (i + k) % size) for i in range(size)])
        for k in range(1, size)
    ]


def place(axes):
    return jnp.reshape(lax.axis_index(axes), (1,))


def body(cotangent, saved_inputs, up_weight, down_weight, block_owner):
    n_x = lax.axis_size("x")
    n_core = lax.axis_size("core")
    n_rep = n_x * n_core
    n_sh = lax.axis_size("sh")
    n_sl = lax.axis_size("sl")
    n_y = lax.axis_size("y")
    n_zh = lax.axis_size("zh")
    tokens, width = cotangent.shape
    block = up_weight.shape[0]

    up_full = lax.all_gather(up_weight, REP, axis=0, tiled=True)
    down_full = lax.all_gather(down_weight, REP, axis=1, tiled=True)

    pair = jnp.stack([saved_inputs.T, cotangent.T])
    spaced = spread(pair, ("sh", "zh"), n_sh * n_zh)
    column = lax.all_gather(spaced, "sl", axis=0, tiled=False)
    full = spread(column, "y", n_y)
    full = full.reshape(n_y, n_sl, n_sh, n_zh, 2, width, tokens)

    inputs_flat, grads_flat, message = arrange(
        full, block_owner, (up_full[:16, :128], down_full[:16, :128])
    )
    message = message.reshape(n_rep, 2, block, tokens)
    owned = lax.all_to_all(message, REP, split_axis=0, concat_axis=0, tiled=True)

    inputs_flat = inputs_flat.reshape(n_rep * block, tokens)
    grads_flat = grads_flat.reshape(n_rep * block, tokens)
    pre_act = lax.dot_general(
        inputs_flat, up_full, (((0,), (0,)), ((), ())), preferred_element_type=jnp.float32
    )
    back_grad = lax.dot_general(
        grads_flat, down_full, (((0,), (1,)), ((), ())), preferred_element_type=jnp.float32
    )
    value, deriv = gelu_pair(pre_act)
    hidden = value.astype(jnp.bfloat16)
    dpre = (back_grad * deriv).astype(jnp.bfloat16)

    both = lax.all_gather(jnp.concatenate([dpre, hidden], axis=1), REP, axis=0, tiled=True)

    partial_grad = lax.dot_general(
        up_full, dpre, (((1,), (1,)), ((), ())), preferred_element_type=jnp.float32
    ).astype(jnp.bfloat16)
    parts = cut(partial_grad.reshape(n_rep, n_y, n_zh, width, tokens), place("y"), n_sh)
    parts = fold(trade(parts, "y"), place("sl"))
    parts = trade(parts, "sl")
    parts = total(parts, owned).reshape(n_sh * n_zh, width, tokens)
    parts = lax.all_to_all(parts, ("sh", "zh"), split_axis=0, concat_axis=0, tiled=True)
    summed = jnp.sum(parts.astype(jnp.float32), axis=0).T
    input_grads = (cotangent.astype(jnp.float32) + summed).astype(jnp.bfloat16)

    weight_grads = block_grads(owned, both.reshape(n_rep, tokens, -1))
    return (input_grads, weight_grads)


def solution(mesh):
    fine = Mesh(mesh.devices.reshape(4, 2, 2, 4, 4, 2), ("x", "core", "sh", "sl", "y", "zh"))
    in_specs = (
        P(REP, SHARD),
        P(REP, SHARD),
        P(REP, SHARD),
        P(SHARD, REP),
        P(),
    )
    out_specs = (P(REP, SHARD), P(None, REP, None, SHARD))
    return jax.shard_map(body, mesh=fine, in_specs=in_specs, out_specs=out_specs, check_vma=False)
```

```python
import math

import jax
import jax.numpy as jnp
from jax import lax
from jax.experimental import pallas as pl
from jax.experimental.pallas import tpu as pltpu
from jax.sharding import Mesh
from jax.sharding import PartitionSpec as P

GELU_SCALE = math.sqrt(2.0 / math.pi)
GELU_CUBIC = 0.044715

REP = ("x", "core")
SHARD = ("sh", "sl", "y", "zh")
SMALL = 24 * 1024 * 1024


def gelu_pair(values):
    tanh_part = jnp.tanh(GELU_SCALE * (values + GELU_CUBIC * values * values * values))
    value = 0.5 * values * (1.0 + tanh_part)
    deriv = 0.5 * (1.0 + tanh_part) + 0.5 * values * (1.0 - tanh_part * tanh_part) * GELU_SCALE * (
        1.0 + 3.0 * GELU_CUBIC * values * values
    )
    return value, deriv


def spread(block, axes, count):
    copies = lax.optimization_barrier(jnp.broadcast_to(block[None], (count,) + block.shape))
    return lax.all_to_all(copies, axes, split_axis=0, concat_axis=0, tiled=True)


def arrange_kernel(owner, gathered, first, second, message, sems):
    _, n_sl, n_sh = gathered.shape[:3]
    n_blocks = n_sl * n_sh
    copies = []
    for j, flat in enumerate((first, second)):
        for r in range(n_blocks):
            b = sum(jnp.where(owner[j, i] == r, i, 0) for i in range(n_blocks))
            copies.append(
                pltpu.make_async_copy(
                    gathered.at[:, lax.rem(b, n_sl), lax.div(b, n_sl), :, j],
                    message.at[r, j],
                    sems.at[len(copies)],
                )
            )
            copies.append(
                pltpu.make_async_copy(
                    gathered.at[:, r % n_sl, r // n_sl, :, j], flat.at[r], sems.at[len(copies)]
                )
            )
    for copy in copies:
        copy.start()
    for copy in copies:
        copy.wait()


def arrange(gathered, owner):
    n_y, n_sl, n_sh, n_zh, _, width, tokens = gathered.shape
    n_blocks = n_sl * n_sh
    out = (n_y, n_zh, width, tokens)
    return pl.pallas_call(
        arrange_kernel,
        in_specs=[
            pl.BlockSpec(memory_space=pltpu.SMEM),
            pl.BlockSpec(memory_space=pl.ANY),
        ],
        out_specs=[pl.BlockSpec(memory_space=pl.ANY)] * 3,
        out_shape=[jax.ShapeDtypeStruct((n_blocks,) + out, gathered.dtype)] * 2
        + [jax.ShapeDtypeStruct((n_blocks, 2) + out, gathered.dtype)],
        scratch_shapes=[pltpu.SemaphoreType.DMA((4 * n_blocks,))],
        compiler_params=pltpu.CompilerParams(vmem_limit_bytes=60 * 1024 * 1024),
        cost_estimate=pl.CostEstimate(
            flops=0, bytes_accessed=8 * gathered.size, transcendentals=0
        ),
    )(owner, gathered)


def cut_kernel(mine, *refs):
    del mine
    count = len(refs) // 2
    for k in range(count):
        refs[count + k][:, 0] = refs[k][:, 0]


def cut(rows, mine, n_sh):
    n_blocks, n_y, *rest = rows.shape
    n_sl = n_blocks // n_sh
    zeros = (0,) * len(rest)
    return pl.pallas_call(
        cut_kernel,
        grid_spec=pltpu.PrefetchScalarGridSpec(
            num_scalar_prefetch=1,
            grid=(n_sh,),
            in_specs=[
                pl.BlockSpec(
                    (n_sl, 1, *rest), lambda i, mine, k=k: (i, lax.rem(mine[0] + k, n_y), *zeros)
                )
                for k in range(n_y)
            ],
            out_specs=[pl.BlockSpec((n_sl, 1, *rest), lambda i, _: (0, i, *zeros))] * n_y,
        ),
        out_shape=[jax.ShapeDtypeStruct((n_sl, n_sh, *rest), rows.dtype)] * n_y,
        compiler_params=pltpu.CompilerParams(vmem_limit_bytes=SMALL),
    )(mine, *([rows] * n_y))


def fold_kernel(count, mine, *refs):
    terms, outs = refs[:count], refs[count:]
    for k in range(len(outs)):
        at = lax.rem(mine[0] + k, len(outs))
        total = terms[0][at].astype(jnp.float32)
        for term in terms[1:]:
            total = total + term[at].astype(jnp.float32)
        outs[k][...] = total.astype(outs[k].dtype)


def fold(terms, mine):
    size, *rest = terms[0].shape
    return pl.pallas_call(
        lambda *refs: fold_kernel(len(terms), *refs),
        grid_spec=pltpu.PrefetchScalarGridSpec(
            num_scalar_prefetch=1,
            grid=(1,),
            in_specs=[pl.BlockSpec((size, *rest), lambda i, _: (0,) * (len(rest) + 1))] * len(terms),
            out_specs=[pl.BlockSpec(tuple(rest), lambda i, _: (0,) * len(rest))] * size,
        ),
        out_shape=[jax.ShapeDtypeStruct(tuple(rest), terms[0].dtype)] * size,
        compiler_params=pltpu.CompilerParams(vmem_limit_bytes=SMALL),
    )(mine, *terms)


def join_kernel(first, second, _, out):
    columns = first.shape[1]
    out[:, :columns] = first[...]
    out[:, columns:] = second[...]


def join(first, second, after):
    rows, columns = first.shape
    return pl.pallas_call(
        join_kernel,
        in_specs=[pl.BlockSpec(memory_space=pltpu.VMEM)] * 2 + [pl.BlockSpec(memory_space=pl.ANY)],
        out_specs=pl.BlockSpec(memory_space=pltpu.VMEM),
        out_shape=jax.ShapeDtypeStruct((rows, 2 * columns), first.dtype),
        compiler_params=pltpu.CompilerParams(vmem_limit_bytes=SMALL),
    )(first, second, after)


def total_kernel(count, *refs):
    total = refs[0][...].astype(jnp.float32)
    for term in refs[1:count]:
        total = total + term[...].astype(jnp.float32)
    refs[-1][...] = total.astype(refs[-1].dtype)


def total(terms, after):
    shape = terms[0].shape
    half = (shape[0] // 2, *shape[1:])
    spec = pl.BlockSpec(half, lambda i: (i,) + (0,) * (len(shape) - 1))
    return pl.pallas_call(
        lambda *refs: total_kernel(len(terms), *refs),
        grid=(2,),
        in_specs=[spec] * len(terms) + [pl.BlockSpec(memory_space=pl.ANY)],
        out_specs=spec,
        out_shape=jax.ShapeDtypeStruct(shape, terms[0].dtype),
        compiler_params=pltpu.CompilerParams(vmem_limit_bytes=SMALL),
    )(*terms, after)


def grads_kernel(pieces, both, out):
    total = None
    for r in range(0, pieces.shape[0], 2):
        left = jnp.concatenate([pieces[r, 0], pieces[r + 1, 0]], axis=1)
        right = jnp.concatenate([both[r], both[r + 1]], axis=0)
        term = jnp.dot(left, right, preferred_element_type=jnp.float32)
        total = term if total is None else total + term
    out[0, 0] = total


def block_grads(pieces, both):
    groups, _, rows, tokens = pieces.shape
    hidden_here = both.shape[2] // 2
    return pl.pallas_call(
        grads_kernel,
        grid=(2,),
        in_specs=[
            pl.BlockSpec((groups, 1, rows, tokens), lambda j: (0, j, 0, 0)),
            pl.BlockSpec((groups, tokens, hidden_here), lambda j: (0, 0, j)),
        ],
        out_specs=pl.BlockSpec((1, 1, rows, hidden_here), lambda j: (j, 0, 0, 0)),
        out_shape=jax.ShapeDtypeStruct((2, 1, rows, hidden_here), jnp.float32),
        compiler_params=pltpu.CompilerParams(vmem_limit_bytes=SMALL),
        cost_estimate=pl.CostEstimate(
            flops=4 * rows * groups * tokens * hidden_here,
            bytes_accessed=4 * rows * groups * tokens + 16 * rows * hidden_here,
            transcendentals=0,
        ),
    )(pieces, both)


def trade(steps, axes):
    size = lax.axis_size(axes)
    return [steps[0]] + [
        lax.ppermute(steps[k], axes, [(i, (i + k) % size) for i in range(size)])
        for k in range(1, size)
    ]


def place(axes):
    return jnp.reshape(lax.axis_index(axes), (1,))


def body(cotangent, saved_inputs, up_weight, down_weight, block_owner):
    n_x = lax.axis_size("x")
    n_core = lax.axis_size("core")
    n_rep = n_x * n_core
    n_sh = lax.axis_size("sh")
    n_sl = lax.axis_size("sl")
    n_y = lax.axis_size("y")
    n_zh = lax.axis_size("zh")
    tokens, width = cotangent.shape
    block = up_weight.shape[0]

    up_full = lax.all_gather(up_weight, REP, axis=0, tiled=True)
    down_full = lax.all_gather(down_weight, REP, axis=1, tiled=True)

    pair = jnp.stack([saved_inputs.T, cotangent.T])
    spaced = spread(pair, ("sh", "zh"), n_sh * n_zh)
    column = lax.all_gather(spaced, "sl", axis=0, tiled=False)
    full = spread(column, "y", n_y)
    full = full.reshape(n_y, n_sl, n_sh, n_zh, 2, width, tokens)

    inputs_flat, grads_flat, message = arrange(full, block_owner)
    message = message.reshape(n_rep, 2, block, tokens)
    owned = lax.all_to_all(message, REP, split_axis=0, concat_axis=0, tiled=True)

    inputs_flat = inputs_flat.reshape(n_rep * block, tokens)
    grads_flat = grads_flat.reshape(n_rep * block, tokens)
    pre_act = lax.dot_general(
        inputs_flat, up_full, (((0,), (0,)), ((), ())), preferred_element_type=jnp.float32
    )
    back_grad = lax.dot_general(
        grads_flat, down_full, (((0,), (1,)), ((), ())), preferred_element_type=jnp.float32
    )
    value, deriv = gelu_pair(pre_act)
    hidden = value.astype(jnp.bfloat16)
    dpre = (back_grad * deriv).astype(jnp.bfloat16)

    partial_grad = lax.dot_general(
        up_full, dpre, (((1,), (1,)), ((), ())), preferred_element_type=jnp.float32
    ).astype(jnp.bfloat16)
    parts = cut(partial_grad.reshape(n_rep, n_y, n_zh, width, tokens), place("y"), n_sh)
    both = lax.all_gather(join(dpre, hidden, parts[0]), REP, axis=0, tiled=True)
    parts = fold(trade(parts, "y"), place("sl"))
    parts = trade(parts, "sl")
    parts = total(parts, owned).reshape(n_sh * n_zh, width, tokens)
    parts = lax.all_to_all(parts, ("sh", "zh"), split_axis=0, concat_axis=0, tiled=True)
    summed = jnp.sum(parts.astype(jnp.float32), axis=0).T
    input_grads = (cotangent.astype(jnp.float32) + summed).astype(jnp.bfloat16)

    weight_grads = block_grads(owned, both.reshape(n_rep, tokens, -1))
    return (input_grads, weight_grads)


def solution(mesh):
    fine = Mesh(mesh.devices.reshape(4, 2, 2, 4, 4, 2), ("x", "core", "sh", "sl", "y", "zh"))
    in_specs = (
        P(REP, SHARD),
        P(REP, SHARD),
        P(REP, SHARD),
        P(SHARD, REP),
        P(),
    )
    out_specs = (P(REP, SHARD), P(None, REP, None, SHARD))
    return jax.shard_map(body, mesh=fine, in_specs=in_specs, out_specs=out_specs, check_vma=False)
```

```python
import math

import jax
import jax.numpy as jnp
from jax import lax
from jax.experimental import pallas as pl
from jax.experimental.pallas import tpu as pltpu
from jax.sharding import Mesh
from jax.sharding import PartitionSpec as P

GELU_SCALE = math.sqrt(2.0 / math.pi)
GELU_CUBIC = 0.044715

REP = ("x", "core")
SHARD = ("sh", "sl", "y", "zh")
SMALL = 24 * 1024 * 1024
LARGE = 57 * 1024 * 1024


def gelu_pair(values):
    tanh_part = jnp.tanh(GELU_SCALE * (values + GELU_CUBIC * values * values * values))
    value = 0.5 * values * (1.0 + tanh_part)
    deriv = 0.5 * (1.0 + tanh_part) + 0.5 * values * (1.0 - tanh_part * tanh_part) * GELU_SCALE * (
        1.0 + 3.0 * GELU_CUBIC * values * values
    )
    return value, deriv


def spread(block, axes, count):
    copies = lax.optimization_barrier(jnp.broadcast_to(block[None], (count,) + block.shape))
    return lax.all_to_all(copies, axes, split_axis=0, concat_axis=0, tiled=True)


def arrange_kernel(owner, gathered, first, second, message):
    _, n_sl, n_sh = gathered.shape[:3]
    n_blocks = n_sl * n_sh
    which, part = pl.program_id(0), pl.program_id(1)
    for j, flat in enumerate((first, second)):

        @pl.when(which == j)
        def _(flat=flat):
            for k in range(n_sl):
                flat[k] = gathered[:, k, part, :, 0]

    for k in range(n_sl):
        target = part * n_sl + k
        b = sum(jnp.where(owner[which, i] == target, i, 0) for i in range(n_blocks))
        message[k, 0] = gathered[:, lax.rem(b, n_sl), lax.div(b, n_sl), :, 0]


def arrange(gathered, owner):
    n_y, n_sl, n_sh, n_zh, _, width, tokens = gathered.shape
    n_blocks = n_sl * n_sh
    out = (n_y, n_zh, width, tokens)
    return pl.pallas_call(
        arrange_kernel,
        grid_spec=pltpu.PrefetchScalarGridSpec(
            num_scalar_prefetch=1,
            grid=(2, n_sh),
            in_specs=[
                pl.BlockSpec(
                    (n_y, n_sl, n_sh, n_zh, 1, width, tokens), lambda j, h, _: (0, 0, 0, 0, j, 0, 0)
                )
            ],
            out_specs=[
                pl.BlockSpec(
                    (n_sl,) + out, lambda j, h, _: (jnp.where(j == 0, h, n_sh - 1), 0, 0, 0, 0)
                ),
                pl.BlockSpec((n_sl,) + out, lambda j, h, _: (jnp.where(j == 0, 0, h), 0, 0, 0, 0)),
                pl.BlockSpec((n_sl, 1) + out, lambda j, h, _: (h, j, 0, 0, 0, 0)),
            ],
        ),
        out_shape=[jax.ShapeDtypeStruct((n_blocks,) + out, gathered.dtype)] * 2
        + [jax.ShapeDtypeStruct((n_blocks, 2) + out, gathered.dtype)],
        compiler_params=pltpu.CompilerParams(vmem_limit_bytes=LARGE),
        cost_estimate=pl.CostEstimate(
            flops=0, bytes_accessed=6 * gathered.size, transcendentals=0
        ),
    )(owner, gathered)


def cut_kernel(mine, *refs):
    del mine
    count = len(refs) // 2
    for k in range(count):
        refs[count + k][:, 0] = refs[k][:, 0]


def cut(rows, mine, n_sh):
    n_blocks, n_y, *rest = rows.shape
    n_sl = n_blocks // n_sh
    zeros = (0,) * len(rest)
    return pl.pallas_call(
        cut_kernel,
        grid_spec=pltpu.PrefetchScalarGridSpec(
            num_scalar_prefetch=1,
            grid=(n_sh,),
            in_specs=[
                pl.BlockSpec(
                    (n_sl, 1, *rest), lambda i, mine, k=k: (i, lax.rem(mine[0] + k, n_y), *zeros)
                )
                for k in range(n_y)
            ],
            out_specs=[pl.BlockSpec((n_sl, 1, *rest), lambda i, _: (0, i, *zeros))] * n_y,
        ),
        out_shape=[jax.ShapeDtypeStruct((n_sl, n_sh, *rest), rows.dtype)] * n_y,
        compiler_params=pltpu.CompilerParams(vmem_limit_bytes=SMALL),
    )(mine, *([rows] * n_y))


def fold_kernel(count, mine, *refs):
    terms, outs = refs[:count], refs[count:]
    for k in range(len(outs)):
        at = lax.rem(mine[0] + k, len(outs))
        total = terms[0][at].astype(jnp.float32)
        for term in terms[1:]:
            total = total + term[at].astype(jnp.float32)
        outs[k][...] = total.astype(outs[k].dtype)


def fold(terms, mine):
    size, *rest = terms[0].shape
    return pl.pallas_call(
        lambda *refs: fold_kernel(len(terms), *refs),
        grid_spec=pltpu.PrefetchScalarGridSpec(
            num_scalar_prefetch=1,
            grid=(1,),
            in_specs=[pl.BlockSpec((size, *rest), lambda i, _: (0,) * (len(rest) + 1))] * len(terms),
            out_specs=[pl.BlockSpec(tuple(rest), lambda i, _: (0,) * len(rest))] * size,
        ),
        out_shape=[jax.ShapeDtypeStruct(tuple(rest), terms[0].dtype)] * size,
        compiler_params=pltpu.CompilerParams(vmem_limit_bytes=SMALL),
    )(mine, *terms)


def total_kernel(count, *refs):
    total = refs[0][...].astype(jnp.float32)
    for term in refs[1:count]:
        total = total + term[...].astype(jnp.float32)
    refs[-1][...] = total.astype(refs[-1].dtype)


def total(terms, after):
    shape = terms[0].shape
    half = (shape[0] // 2, *shape[1:])
    spec = pl.BlockSpec(half, lambda i: (i,) + (0,) * (len(shape) - 1))
    return pl.pallas_call(
        lambda *refs: total_kernel(len(terms), *refs),
        grid=(2,),
        in_specs=[spec] * len(terms) + [pl.BlockSpec(memory_space=pl.ANY)],
        out_specs=spec,
        out_shape=jax.ShapeDtypeStruct(shape, terms[0].dtype),
        compiler_params=pltpu.CompilerParams(vmem_limit_bytes=SMALL),
    )(*terms, after)


def grads_kernel(pieces, both, out):
    total = None
    for r in range(0, pieces.shape[0], 2):
        left = jnp.concatenate([pieces[r, 0], pieces[r + 1, 0]], axis=1)
        right = jnp.concatenate([both[r], both[r + 1]], axis=0)
        term = jnp.dot(left, right, preferred_element_type=jnp.float32)
        total = term if total is None else total + term
    out[0, 0] = total


def block_grads(pieces, both):
    groups, _, rows, tokens = pieces.shape
    hidden_here = both.shape[2] // 2
    return pl.pallas_call(
        grads_kernel,
        grid=(2,),
        in_specs=[
            pl.BlockSpec((groups, 1, rows, tokens), lambda j: (0, j, 0, 0)),
            pl.BlockSpec((groups, tokens, hidden_here), lambda j: (0, 0, j)),
        ],
        out_specs=pl.BlockSpec((1, 1, rows, hidden_here), lambda j: (j, 0, 0, 0)),
        out_shape=jax.ShapeDtypeStruct((2, 1, rows, hidden_here), jnp.float32),
        compiler_params=pltpu.CompilerParams(vmem_limit_bytes=LARGE),
        cost_estimate=pl.CostEstimate(
            flops=4 * rows * groups * tokens * hidden_here,
            bytes_accessed=4 * rows * groups * tokens + 16 * rows * hidden_here,
            transcendentals=0,
        ),
    )(pieces, both)


def trade(steps, axes):
    size = lax.axis_size(axes)
    came = list(steps)
    for k in sorted(range(1, size), key=lambda k: -min(k, size - k)):
        came[k] = lax.ppermute(steps[k], axes, [(i, (i + k) % size) for i in range(size)])
    return came


def place(axes):
    return jnp.reshape(lax.axis_index(axes), (1,))


def body(cotangent, saved_inputs, up_weight, down_weight, block_owner):
    n_x = lax.axis_size("x")
    n_core = lax.axis_size("core")
    n_rep = n_x * n_core
    n_sh = lax.axis_size("sh")
    n_sl = lax.axis_size("sl")
    n_y = lax.axis_size("y")
    n_zh = lax.axis_size("zh")
    tokens, width = cotangent.shape
    block = up_weight.shape[0]

    up_full = lax.all_gather(up_weight, REP, axis=0, tiled=True)
    down_full = lax.all_gather(down_weight, REP, axis=1, tiled=True)

    pair = jnp.stack([saved_inputs.T, cotangent.T])
    spaced = spread(pair, ("sh", "zh"), n_sh * n_zh)
    column = lax.all_gather(spaced, "sl", axis=0, tiled=False)
    full = spread(column, "y", n_y)
    full = full.reshape(n_y, n_sl, n_sh, n_zh, 2, width, tokens)

    inputs_flat, grads_flat, message = arrange(full, block_owner)
    message = message.reshape(n_rep, 2, block, tokens)
    owned = lax.all_to_all(message, REP, split_axis=0, concat_axis=0, tiled=True)

    inputs_flat = inputs_flat.reshape(n_rep * block, tokens)
    grads_flat = grads_flat.reshape(n_rep * block, tokens)
    pre_act = lax.dot_general(
        inputs_flat, up_full, (((0,), (0,)), ((), ())), preferred_element_type=jnp.float32
    )
    back_grad = lax.dot_general(
        grads_flat, down_full, (((0,), (1,)), ((), ())), preferred_element_type=jnp.float32
    )
    value, deriv = gelu_pair(pre_act)
    hidden = value.astype(jnp.bfloat16)
    dpre = (back_grad * deriv).astype(jnp.bfloat16)

    both = lax.all_gather(jnp.concatenate([dpre, hidden], axis=1), REP, axis=0, tiled=True)

    partial_grad = lax.dot_general(
        up_full, dpre, (((1,), (1,)), ((), ())), preferred_element_type=jnp.float32
    ).astype(jnp.bfloat16)
    parts = cut(partial_grad.reshape(n_rep, n_y, n_zh, width, tokens), place("y"), n_sh)
    parts = fold(trade(parts, "y"), place("sl"))
    parts = trade(parts, "sl")
    parts = total(parts, owned).reshape(n_sh * n_zh, width, tokens)
    parts = lax.all_to_all(parts, ("sh", "zh"), split_axis=0, concat_axis=0, tiled=True)
    summed = jnp.sum(parts.astype(jnp.float32), axis=0).T
    input_grads = (cotangent.astype(jnp.float32) + summed).astype(jnp.bfloat16)

    weight_grads = block_grads(owned, both.reshape(n_rep, tokens, -1))
    return (input_grads, weight_grads)


def solution(mesh):
    fine = Mesh(mesh.devices.reshape(4, 2, 2, 4, 4, 2), ("x", "core", "sh", "sl", "y", "zh"))
    in_specs = (
        P(REP, SHARD),
        P(REP, SHARD),
        P(REP, SHARD),
        P(SHARD, REP),
        P(),
    )
    out_specs = (P(REP, SHARD), P(None, REP, None, SHARD))
    return jax.shard_map(body, mesh=fine, in_specs=in_specs, out_specs=out_specs, check_vma=False)
```

```python
import math

import jax
import jax.numpy as jnp
from jax import lax
from jax.experimental import pallas as pl
from jax.experimental.pallas import tpu as pltpu
from jax.sharding import Mesh
from jax.sharding import PartitionSpec as P

GELU_SCALE = math.sqrt(2.0 / math.pi)
GELU_CUBIC = 0.044715

REP = ("x", "core")
SHARD = ("sh", "sl", "y", "zh")
SMALL = 24 * 1024 * 1024
LARGE = 56 * 1024 * 1024


def gelu_pair(values):
    tanh_part = jnp.tanh(GELU_SCALE * (values + GELU_CUBIC * values * values * values))
    value = 0.5 * values * (1.0 + tanh_part)
    deriv = 0.5 * (1.0 + tanh_part) + 0.5 * values * (1.0 - tanh_part * tanh_part) * GELU_SCALE * (
        1.0 + 3.0 * GELU_CUBIC * values * values
    )
    return value, deriv


def spread(block, axes, count):
    copies = lax.optimization_barrier(jnp.broadcast_to(block[None], (count,) + block.shape))
    return lax.all_to_all(copies, axes, split_axis=0, concat_axis=0, tiled=True)


def arrange_kernel(owner, gathered, first, second, message):
    _, n_sl, n_sh = gathered.shape[:3]
    n_blocks = n_sl * n_sh
    which, part = pl.program_id(0), pl.program_id(1)
    for j, flat in enumerate((first, second)):

        @pl.when(which == j)
        def _(flat=flat):
            for k in range(n_sl):
                flat[k] = gathered[:, k, part, :, 0]

    for k in range(n_sl):
        target = part * n_sl + k
        b = sum(jnp.where(owner[which, i] == target, i, 0) for i in range(n_blocks))
        message[k, 0] = gathered[:, lax.rem(b, n_sl), lax.div(b, n_sl), :, 0]


def arrange(gathered, owner):
    n_y, n_sl, n_sh, n_zh, _, width, tokens = gathered.shape
    n_blocks = n_sl * n_sh
    out = (n_y, n_zh, width, tokens)
    return pl.pallas_call(
        arrange_kernel,
        grid_spec=pltpu.PrefetchScalarGridSpec(
            num_scalar_prefetch=1,
            grid=(2, n_sh),
            in_specs=[
                pl.BlockSpec(
                    (n_y, n_sl, n_sh, n_zh, 1, width, tokens), lambda j, h, _: (0, 0, 0, 0, j, 0, 0)
                )
            ],
            out_specs=[
                pl.BlockSpec(
                    (n_sl,) + out, lambda j, h, _: (jnp.where(j == 0, h, n_sh - 1), 0, 0, 0, 0)
                ),
                pl.BlockSpec((n_sl,) + out, lambda j, h, _: (jnp.where(j == 0, 0, h), 0, 0, 0, 0)),
                pl.BlockSpec((n_sl, 1) + out, lambda j, h, _: (h, j, 0, 0, 0, 0)),
            ],
        ),
        out_shape=[jax.ShapeDtypeStruct((n_blocks,) + out, gathered.dtype)] * 2
        + [jax.ShapeDtypeStruct((n_blocks, 2) + out, gathered.dtype)],
        compiler_params=pltpu.CompilerParams(vmem_limit_bytes=LARGE),
        cost_estimate=pl.CostEstimate(
            flops=0, bytes_accessed=6 * gathered.size, transcendentals=0
        ),
    )(owner, gathered)


def cut_kernel(mine, *refs):
    del mine
    count = len(refs) // 2
    for k in range(count):
        refs[count + k][:, 0] = refs[k][:, 0]


def cut(rows, mine, n_sh):
    n_blocks, n_y, *rest = rows.shape
    n_sl = n_blocks // n_sh
    zeros = (0,) * len(rest)
    return pl.pallas_call(
        cut_kernel,
        grid_spec=pltpu.PrefetchScalarGridSpec(
            num_scalar_prefetch=1,
            grid=(n_sh,),
            in_specs=[
                pl.BlockSpec(
                    (n_sl, 1, *rest), lambda i, mine, k=k: (i, lax.rem(mine[0] + k, n_y), *zeros)
                )
                for k in range(n_y)
            ],
            out_specs=[pl.BlockSpec((n_sl, 1, *rest), lambda i, _: (0, i, *zeros))] * n_y,
        ),
        out_shape=[jax.ShapeDtypeStruct((n_sl, n_sh, *rest), rows.dtype)] * n_y,
        compiler_params=pltpu.CompilerParams(vmem_limit_bytes=SMALL),
    )(mine, *([rows] * n_y))


def fold_kernel(count, mine, *refs):
    terms, outs = refs[:count], refs[count:]
    for k in range(len(outs)):
        at = lax.rem(mine[0] + k, len(outs))
        total = terms[0][at].astype(jnp.float32)
        for term in terms[1:]:
            total = total + term[at].astype(jnp.float32)
        outs[k][...] = total.astype(outs[k].dtype)


def fold(terms, mine):
    size, *rest = terms[0].shape
    return pl.pallas_call(
        lambda *refs: fold_kernel(len(terms), *refs),
        grid_spec=pltpu.PrefetchScalarGridSpec(
            num_scalar_prefetch=1,
            grid=(1,),
            in_specs=[pl.BlockSpec((size, *rest), lambda i, _: (0,) * (len(rest) + 1))] * len(terms),
            out_specs=[pl.BlockSpec(tuple(rest), lambda i, _: (0,) * len(rest))] * size,
        ),
        out_shape=[jax.ShapeDtypeStruct(tuple(rest), terms[0].dtype)] * size,
        compiler_params=pltpu.CompilerParams(vmem_limit_bytes=SMALL),
    )(mine, *terms)


def join_kernel(first, second, _, out):
    columns = first.shape[1]
    out[:, :columns] = first[...]
    out[:, columns:] = second[...]


def join(first, second, after):
    rows, columns = first.shape
    return pl.pallas_call(
        join_kernel,
        in_specs=[pl.BlockSpec(memory_space=pltpu.VMEM)] * 2 + [pl.BlockSpec(memory_space=pl.ANY)],
        out_specs=pl.BlockSpec(memory_space=pltpu.VMEM),
        out_shape=jax.ShapeDtypeStruct((rows, 2 * columns), first.dtype),
        compiler_params=pltpu.CompilerParams(vmem_limit_bytes=SMALL),
    )(first, second, after)


def total_kernel(count, *refs):
    total = refs[0][...].astype(jnp.float32)
    for term in refs[1:count]:
        total = total + term[...].astype(jnp.float32)
    refs[-1][...] = total.astype(refs[-1].dtype)


def total(terms, after):
    shape = terms[0].shape
    half = (shape[0] // 2, *shape[1:])
    spec = pl.BlockSpec(half, lambda i: (i,) + (0,) * (len(shape) - 1))
    return pl.pallas_call(
        lambda *refs: total_kernel(len(terms), *refs),
        grid=(2,),
        in_specs=[spec] * len(terms) + [pl.BlockSpec(memory_space=pl.ANY)],
        out_specs=spec,
        out_shape=jax.ShapeDtypeStruct(shape, terms[0].dtype),
        compiler_params=pltpu.CompilerParams(vmem_limit_bytes=SMALL),
    )(*terms, after)


def grads_kernel(pieces, both, out):
    total = None
    for r in range(0, pieces.shape[0], 2):
        left = jnp.concatenate([pieces[r, 0], pieces[r + 1, 0]], axis=1)
        right = jnp.concatenate([both[r], both[r + 1]], axis=0)
        term = jnp.dot(left, right, preferred_element_type=jnp.float32)
        total = term if total is None else total + term
    out[0, 0] = total


def block_grads(pieces, both):
    groups, _, rows, tokens = pieces.shape
    hidden_here = both.shape[2] // 2
    return pl.pallas_call(
        grads_kernel,
        grid=(2,),
        in_specs=[
            pl.BlockSpec((groups, 1, rows, tokens), lambda j: (0, j, 0, 0)),
            pl.BlockSpec((groups, tokens, hidden_here), lambda j: (0, 0, j)),
        ],
        out_specs=pl.BlockSpec((1, 1, rows, hidden_here), lambda j: (j, 0, 0, 0)),
        out_shape=jax.ShapeDtypeStruct((2, 1, rows, hidden_here), jnp.float32),
        compiler_params=pltpu.CompilerParams(vmem_limit_bytes=LARGE),
        cost_estimate=pl.CostEstimate(
            flops=4 * rows * groups * tokens * hidden_here,
            bytes_accessed=4 * rows * groups * tokens + 16 * rows * hidden_here,
            transcendentals=0,
        ),
    )(pieces, both)


def trade(steps, axes):
    size = lax.axis_size(axes)
    came = list(steps)
    for k in sorted(range(1, size), key=lambda k: -min(k, size - k)):
        came[k] = lax.ppermute(steps[k], axes, [(i, (i + k) % size) for i in range(size)])
    return came


def place(axes):
    return jnp.reshape(lax.axis_index(axes), (1,))


def body(cotangent, saved_inputs, up_weight, down_weight, block_owner):
    n_x = lax.axis_size("x")
    n_core = lax.axis_size("core")
    n_rep = n_x * n_core
    n_sh = lax.axis_size("sh")
    n_sl = lax.axis_size("sl")
    n_y = lax.axis_size("y")
    n_zh = lax.axis_size("zh")
    tokens, width = cotangent.shape
    block = up_weight.shape[0]

    up_full = lax.all_gather(up_weight, REP, axis=0, tiled=True)
    down_full = lax.all_gather(down_weight, REP, axis=1, tiled=True)

    pair = jnp.stack([saved_inputs.T, cotangent.T])
    spaced = spread(pair, ("sh", "zh"), n_sh * n_zh)
    column = lax.all_gather(spaced, "sl", axis=0, tiled=False)
    full = spread(column, "y", n_y)
    full = full.reshape(n_y, n_sl, n_sh, n_zh, 2, width, tokens)

    inputs_flat, grads_flat, message = arrange(full, block_owner)
    message = message.reshape(n_rep, 2, block, tokens)
    owned = lax.all_to_all(message, REP, split_axis=0, concat_axis=0, tiled=True)

    inputs_flat = inputs_flat.reshape(n_rep * block, tokens)
    grads_flat = grads_flat.reshape(n_rep * block, tokens)
    pre_act = lax.dot_general(
        inputs_flat, up_full, (((0,), (0,)), ((), ())), preferred_element_type=jnp.float32
    )
    back_grad = lax.dot_general(
        grads_flat, down_full, (((0,), (1,)), ((), ())), preferred_element_type=jnp.float32
    )
    value, deriv = gelu_pair(pre_act)
    hidden = value.astype(jnp.bfloat16)
    dpre = (back_grad * deriv).astype(jnp.bfloat16)

    partial_grad = lax.dot_general(
        up_full, dpre, (((1,), (1,)), ((), ())), preferred_element_type=jnp.float32
    ).astype(jnp.bfloat16)
    parts = cut(partial_grad.reshape(n_rep, n_y, n_zh, width, tokens), place("y"), n_sh)
    both = lax.all_gather(join(dpre, hidden, parts[0]), REP, axis=0, tiled=True)
    parts = fold(trade(parts, "y"), place("sl"))
    parts = trade(parts, "sl")
    parts = total(parts, owned).reshape(n_sh * n_zh, width, tokens)
    parts = lax.all_to_all(parts, ("sh", "zh"), split_axis=0, concat_axis=0, tiled=True)
    summed = jnp.sum(parts.astype(jnp.float32), axis=0).T
    input_grads = (cotangent.astype(jnp.float32) + summed).astype(jnp.bfloat16)

    weight_grads = block_grads(owned, both.reshape(n_rep, tokens, -1))
    return (input_grads, weight_grads)


def solution(mesh):
    fine = Mesh(mesh.devices.reshape(4, 2, 2, 4, 4, 2), ("x", "core", "sh", "sl", "y", "zh"))
    in_specs = (
        P(REP, SHARD),
        P(REP, SHARD),
        P(REP, SHARD),
        P(SHARD, REP),
        P(),
    )
    out_specs = (P(REP, SHARD), P(None, REP, None, SHARD))
    return jax.shard_map(body, mesh=fine, in_specs=in_specs, out_specs=out_specs, check_vma=False)
```
